512 devices in a mesh: gx: 16 (over z), gy: 8 (over y, core), gz: 4 (over x).
Axes of the slice: x: 4, y: 4, z: 16, core: 2. Of those that a mesh axis runs over, the one named last changes fastest.
Arguments:
- adjoint: bfloat16 [6, 32, 128, 1024], P(None, 'gz', 'gx', 'gy'), may hold values from -6 to 6
- linearized: bfloat16 [18, 32, 128, 1024], P(None, 'gz', 'gx', 'gy'), may hold values from -24 to 24
- stiffness: bfloat16 [32, 128, 1024], P('gz', 'gx', 'gy'), may hold values from 0.5 to 8
- anchor: float32 [32, 128, 1024], P('gz', 'gx', 'gy'), may hold values from 0.5 to 2
- target_tile: int32 [16, 8, 1024, 1], P('gx', 'gy'), may hold values from 0 to 127, as said below
- target_row: int32 [16, 8, 1024], P('gx', 'gy'), may hold values from 0 to 254
- target_col: int32 [16, 8, 1024], P('gx', 'gy'), may hold values from 0 to 126
- offsets: float32 [2, 16, 8, 1024], P(None, 'gx', 'gy'), may hold values from 0 to 1
Outputs:
- deformation_adjoint: float32 [3, 32, 128, 1024], P(None, 'gz', 'gx', 'gy')
- dem_gradient: float32 [2048, 2048], P('gy', 'gx')
The draws below stay inside these ranges and needn't reach their ends.
Inputs may be any that keep to these rules, and one draw needn't show every extreme that they name: `target_tile`: A ground node of block (bx, by) names the tile of that block, bx * 8 + by, or the tile one block further along x, along y, or along both.
All inputs are finite; a program needn't handle non-finite values.
Results may differ from the reference program's by a relative error of at most 0.0005.
Values may be sent and summed in bfloat16 or wider, within the bound.
A program may use at most 64 MiB of HBM per device.

```python
import math
import jax
import jax.numpy as jnp

NVAR = 6
DEVICE_NODES_X = 8
DEVICE_NODES_Y = 128
TILE_ROWS = 256
TILE_COLUMNS = 128
ITERS = 3
MESH_NODES_X = 128
MESH_NODES_Y = 1024
NZ = 32
N_GX = 16
N_GY = 8


def draw_stiffness(key, part):
    key = jax.random.fold_in(key, 7)
    uniform_part = jax.random.uniform(key, (NZ, MESH_NODES_X, MESH_NODES_Y), jnp.float32)
    spread = jnp.exp(jnp.log(0.5) + uniform_part * jnp.log(4.0))
    growth = 1.0 + 2.0 * jnp.arange(MESH_NODES_X, dtype=jnp.float32) / (MESH_NODES_X - 1)
    scaled = spread * growth[None, :, None]
    return scaled.astype(jnp.bfloat16)


def ground_map(key):
    keys = jax.random.split(key, 5)
    row_offset = jax.random.randint(keys[0], (), 1, TILE_ROWS // 2 + 1)
    column_offset = jax.random.randint(keys[1], (), 1, TILE_COLUMNS // 2 + 1)
    row_slope = jax.random.randint(keys[2], (), 0, TILE_ROWS // 4 + 1)
    column_slope = jax.random.randint(keys[3], (), 0, TILE_COLUMNS // 4 + 1)
    random_perturbation = jax.random.randint(keys[4], (2, N_GX, N_GY, DEVICE_NODES_X * DEVICE_NODES_Y), 0, 2)
    block_x = jnp.arange(N_GX, dtype=jnp.int32)[:, None, None]
    block_y = jnp.arange(N_GY, dtype=jnp.int32)[None, :, None]
    entry = jnp.arange(DEVICE_NODES_X * DEVICE_NODES_Y, dtype=jnp.int32)[None, None, :]
    node_position_x = block_x * DEVICE_NODES_X + entry // DEVICE_NODES_Y
    node_position_y = block_y * DEVICE_NODES_Y + entry % DEVICE_NODES_Y
    elevation_row = node_position_y * TILE_ROWS // DEVICE_NODES_Y + row_offset + node_position_x * row_slope // MESH_NODES_X + random_perturbation[0]
    elevation_column = node_position_x * TILE_COLUMNS // DEVICE_NODES_X + column_offset + node_position_y * column_slope // MESH_NODES_Y + random_perturbation[1]
    elevation_row = jnp.minimum(elevation_row, TILE_ROWS * N_GY - 2)
    elevation_column = jnp.minimum(elevation_column, TILE_COLUMNS * N_GX - 2)
    tile_row_index = elevation_row // TILE_ROWS
    tile_column_index = elevation_column // TILE_COLUMNS
    row_within_tile = jnp.minimum(elevation_row - tile_row_index * TILE_ROWS, TILE_ROWS - 2)
    column_within_tile = jnp.minimum(elevation_column - tile_column_index * TILE_COLUMNS, TILE_COLUMNS - 2)
    tiles = tile_column_index * N_GY + tile_row_index
    return (tiles.astype(jnp.int32), row_within_tile.astype(jnp.int32), column_within_tile.astype(jnp.int32))


def draw_target_tile(key, part):
    tiles, row_within_tile, column_within_tile = ground_map(key)
    return tiles[..., None]


def draw_target_row(key, part):
    tiles, row_within_tile, column_within_tile = ground_map(key)
    return row_within_tile


def draw_target_col(key, part):
    tiles, row_within_tile, column_within_tile = ground_map(key)
    return column_within_tile


def shard_levels(key, shape, cuts, low, high):
    loudness = 1.0
    for dim, shards_of in cuts:
        heights = jax.random.uniform(jax.random.fold_in(jax.random.fold_in(key, 6), dim), (shards_of,), jnp.float32, low / len(cuts), high / len(cuts))
        loudness = loudness * jnp.repeat(jnp.exp(heights), shape[dim] // shards_of).reshape((-1,) + (1,) * (len(shape) - 1 - dim))
    return loudness


def normal_values(rng, dims, scale, limit, pieces=(), kind=jnp.bfloat16):
    level = shard_levels(rng, dims, pieces, -0.22, 0.18) if pieces else 1.0
    drawn = jax.random.normal(rng, dims, jnp.float32) * scale * level
    return jnp.minimum(jnp.maximum(drawn, -limit), limit).astype(kind)


def setup_inputs(seed: int = 0) -> dict:
    seeds = jax.random.split(jax.random.key(seed), 9)
    return {
        "adjoint": normal_values(seeds[0], (NVAR, NZ, MESH_NODES_X, MESH_NODES_Y), 1.0, 6.0, ((1, 4), (2, 16), (3, 8))),
        "linearized": normal_values(seeds[1], (3 * NVAR, NZ, MESH_NODES_X, MESH_NODES_Y), 4.0, 24.0, ((1, 4), (2, 16), (3, 8))),
        "stiffness": draw_stiffness(jax.random.fold_in(seeds[8], 71), 0),
        "anchor": jnp.clip(jnp.exp(math.log(2.0) - 1.3862944 * jax.random.uniform(seeds[3], (NZ, MESH_NODES_X, MESH_NODES_Y), jnp.float32) ** shard_levels(seeds[3], (NZ, MESH_NODES_X, MESH_NODES_Y), ((0, 4), (1, 16), (2, 8)), -0.2, 0.2)), 0.5, 2.0),
        "target_tile": draw_target_tile(jax.random.fold_in(seeds[8], 71), 0),
        "target_row": draw_target_row(jax.random.fold_in(seeds[8], 71), 0),
        "target_col": draw_target_col(jax.random.fold_in(seeds[8], 71), 0),
        "offsets": jnp.clip(1.0 * jax.random.uniform(seeds[7], (2, N_GX, N_GY, DEVICE_NODES_X * DEVICE_NODES_Y), jnp.float32) ** shard_levels(seeds[7], (2, N_GX, N_GY, DEVICE_NODES_X * DEVICE_NODES_Y), ((1, 16), (2, 8)), -0.2, 0.2), 0.0, 1.0),
    }


stabilizer = 0.25
element_bound = 2.75
spectrum_ratio = 30.0
corner_bits = ((0, 0, 0), (0, 0, 1), (0, 1, 0), (0, 1, 1), (1, 0, 0), (1, 0, 1), (1, 1, 0), (1, 1, 1))


def axis_valid(first_lower, length, global_len):
    lower_ids = first_lower + jnp.arange(length, dtype=jnp.int32)
    return ((lower_ids >= 0) & (lower_ids <= global_len - 2)).astype(jnp.float32)


def box_mask(firsts, counts, totals):
    along_z = axis_valid(firsts[0], counts[0], totals[0])
    along_x = axis_valid(firsts[1], counts[1], totals[1])
    along_y = axis_valid(firsts[2], counts[2], totals[2])
    return along_z[:, None, None] * along_x[None, :, None] * along_y[None, None, :]


def corner_view(values_in, corner, extent):
    return values_in[:, corner[0]:corner[0] + extent[0], corner[1]:corner[1] + extent[1], corner[2]:corner[2] + extent[2]]


def node_view(values_in, corner, extent):
    return values_in[:, 1 - corner[0]:1 - corner[0] + extent[0], 1 - corner[1]:1 - corner[1] + extent[1], 1 - corner[2]:1 - corner[2] + extent[2]]


def corner_signs(corner):
    return (2.0 * corner[1] - 1.0, 2.0 * corner[2] - 1.0, 2.0 * corner[0] - 1.0)


def element_sense(node_values, linear, mask):
    extent = (node_values.shape[1] - 1, node_values.shape[2] - 1, node_values.shape[3] - 1)
    average = corner_view(node_values, corner_bits[0], extent)
    for corner in corner_bits[1:]:
        average = average + corner_view(node_values, corner, extent)
    average = average * 0.125
    senses = []
    for direction in range(3):
        summed = linear[direction].astype(jnp.float32) * average[0]
        for variable in range(1, average.shape[0]):
            summed = summed + linear[3 * variable + direction].astype(jnp.float32) * average[variable]
        senses.append(summed * mask)
    return jnp.stack(senses)


def transpose_gradient(element_terms, extent):
    result = jnp.zeros((3, extent[0], extent[1], extent[2]), jnp.float32)
    for corner in corner_bits:
        sign_set = corner_signs(corner)
        sign_column = jnp.array(sign_set, dtype=jnp.float32)[:, None, None, None]
        result = result + 0.25 * sign_column * node_view(element_terms, corner, extent)
    return result


def node_total(weights, extent):
    result = jnp.zeros((extent[0], extent[1], extent[2]), jnp.float32)
    for corner in corner_bits:
        result = result + node_view(weights[None], corner, extent)[0]
    return result


def node_forces(padded, weights, extent):
    elem_span = (extent[0] + 1, extent[1] + 1, extent[2] + 1)
    local_weights = weights[:elem_span[0], :elem_span[1], :elem_span[2]]
    corners = [corner_view(padded, corner, elem_span) for corner in corner_bits]
    mean_disp = corners[0]
    for position in range(1, 8):
        mean_disp = mean_disp + corners[position]
    mean_disp = mean_disp * 0.125
    gradient = []
    for direction in range(3):
        summed = 0.25 * corner_signs(corner_bits[0])[direction] * corners[0]
        for position in range(1, 8):
            summed = summed + 0.25 * corner_signs(corner_bits[position])[direction] * corners[position]
        gradient.append(summed)
    trace_term = gradient[0][0] + gradient[1][1] + gradient[2][2]
    stress = []
    for direction in range(3):
        stress_rows = []
        for component in range(3):
            entry_value = gradient[direction][component] + gradient[component][direction]
            if component == direction:
                entry_value = entry_value + trace_term
            stress_rows.append(local_weights * entry_value)
        stress.append(jnp.stack(stress_rows))
    result = jnp.zeros((3, extent[0], extent[1], extent[2]), jnp.float32)
    for position in range(8):
        sign_set = corner_signs(corner_bits[position])
        corner_force = 0.25 * (sign_set[0] * stress[0] + sign_set[1] * stress[1] + sign_set[2] * stress[2])
        corner_force = corner_force + stabilizer * local_weights * (corners[position] - mean_disp)
        result = result + node_view(corner_force, corner_bits[position], extent)
    return result


def reference(adjoint, linearized, stiffness, anchor, target_tile, target_row, target_col, offsets):
    extent = (NZ, MESH_NODES_X, MESH_NODES_Y)
    border = ((0, 0), (1, 1), (1, 1), (1, 1))
    node_values = jnp.pad(adjoint.astype(jnp.float32), border)
    element_terms = element_sense(node_values[:, 1:, 1:, 1:], linearized, box_mask((0, 0, 0), extent, extent))
    element_terms = jnp.pad(element_terms, ((0, 0), (1, 0), (1, 0), (1, 0)))
    coordinate_gradient = transpose_gradient(element_terms, extent)
    weights = jnp.pad(stiffness.astype(jnp.float32), 1) * box_mask((-1, -1, -1), (NZ + 2, MESH_NODES_X + 2, MESH_NODES_Y + 2), extent)
    top_bound = jnp.max(anchor + element_bound * node_total(weights, extent))
    low_bound = top_bound / spectrum_ratio
    center = 0.5 * (top_bound + low_bound)
    half_width = 0.5 * (top_bound - low_bound)
    ratio_term = center / half_width
    rho_now = 1.0 / ratio_term
    deformation_adjoint = jnp.zeros_like(coordinate_gradient)
    residual = coordinate_gradient
    direction = residual / center
    for sweep_step in range(ITERS):
        applied = anchor[None] * direction + node_forces(jnp.pad(direction, border), weights, extent)
        deformation_adjoint = deformation_adjoint + direction
        residual = residual - applied
        rho_next = 1.0 / (2.0 * ratio_term - rho_now)
        direction = rho_next * rho_now * direction + (2.0 * rho_next / half_width) * residual
        rho_now = rho_next
    levels = jnp.arange(NZ, dtype=jnp.float32)
    blending = (NZ - 1 - levels) / (NZ - 1)
    column = jnp.sum(blending[:, None, None] * deformation_adjoint[2], axis=0)
    ground_surface = column.reshape(N_GX, DEVICE_NODES_X, N_GY, DEVICE_NODES_Y).transpose(0, 2, 1, 3).reshape(-1)
    tile_ids = target_tile.reshape(-1)
    row_index_at = (tile_ids % N_GY) * TILE_ROWS + target_row.reshape(-1)
    column_index_at = (tile_ids // N_GY) * TILE_COLUMNS + target_col.reshape(-1)
    row_fraction = offsets[0].reshape(-1)
    column_fraction = offsets[1].reshape(-1)
    elevation_field = jnp.zeros((TILE_ROWS * N_GY, TILE_COLUMNS * N_GX), jnp.float32)
    elevation_field = elevation_field.at[row_index_at, column_index_at].add(ground_surface * ((1.0 - row_fraction) * (1.0 - column_fraction)))
    elevation_field = elevation_field.at[row_index_at, column_index_at + 1].add(ground_surface * ((1.0 - row_fraction) * column_fraction))
    elevation_field = elevation_field.at[row_index_at + 1, column_index_at].add(ground_surface * (row_fraction * (1.0 - column_fraction)))
    elevation_field = elevation_field.at[row_index_at + 1, column_index_at + 1].add(ground_surface * (row_fraction * column_fraction))
    return deformation_adjoint, elevation_field
```

```python
import functools
import itertools

import jax
import jax.numpy as jnp
from jax import lax
from jax.experimental import pallas as pl
from jax.experimental.pallas import tpu as pltpu
from jax.sharding import PartitionSpec as P

MESH = pl.DeviceIdType.MESH
F32, BF16 = jnp.float32, jnp.bfloat16
NX, NY, NZ = 16, 8, 4
BZ, BX, BY = 8, 8, 128
TILE_ROWS, TILE_COLUMNS = 256, 128
VARIABLES = 6
SZ, WZ, AZ = 13, 11, 9
EDGE_Z, INNER_Z = (5, 6, 7, 0, 1), (2, 3, 4)

NEAR = [d for d in itertools.product((-1, 0, 1), repeat=3) if d != (0, 0, 0)]
PLANE = sorted(
    [(b, c) for b in range(NY) for c in range(NZ) if (b, c) != (0, 0)],
    key=lambda d: -(min(d[0], NY - d[0]) // 2 + min(d[1], NZ - d[1])),
)
GROUND = [(a, b, c) for a in (0, 1) for b in (0, 1) for c in range(NZ)]


def near_index(d):
    return (d[0] + 1) * 9 + (d[1] + 1) * 3 + d[2] + 1


def guarded(condition, act):
    if condition is None:
        act()
    else:
        pl.when(condition)(act)


def rows_between(dx):
    if dx == 0:
        return pl.ds(0, 8), pl.ds(0, 8)
    return (pl.ds(4, 4), pl.ds(12, 4)) if dx == 1 else (pl.ds(0, 4), pl.ds(8, 4))


def layers_between(dz, below, above):
    if dz == 0:
        return pl.ds(0, BZ), pl.ds(below, BZ)
    if dz == 1:
        return pl.ds(BZ - below, below), pl.ds(0, below)
    return pl.ds(0, above), pl.ds(below + BZ, above)


def kernel(
    adj_h, lin_h, stiff_h, anchor_h, tile_h, row_h, col_h, off_h,
    def_o, dem_o,
    adj_v, lin_v, stiff_v, anchor_v, tile_v, row_v, col_v, off_v,
    AX, PA, PAE, WX, PW, PWE, EX, PS, PSE, TE, W16, DG, G, K1, K2, CE, P1, P2, P3,
    RH, RL, CV,
    load_sem, w_send, w_recv, a_send, a_recv, t_send, t_recv, s_send, s_recv,
    e_send, e_recv, p1_send, p1_recv, p2_send, p2_recv, p3_send, p3_recv,
):
    gx, gy, gz = lax.axis_index("gx"), lax.axis_index("gy"), lax.axis_index("gz")

    def at(dx, dy, dz):
        return (gx + dx, lax.rem(gy + dy + NY, NY), lax.rem(gz + dz + NZ, NZ))

    first, last = gx == 0, gx == NX - 1
    not_first, not_last = gx > 0, gx < NX - 1
    can_send = {0: None, 1: not_last, -1: not_first}
    can_receive = {0: None, 1: not_first, -1: not_last}

    barrier = pltpu.get_barrier_semaphore()

    def greet(device):
        pl.semaphore_signal(barrier, inc=1, device_id=device, device_id_type=MESH)

    def greet_x(dx):
        for dy in (-1, 0, 1):
            for dz in (-1, 0, 1):
                greet(at(dx, dy, dz))

    for b, c in PLANE:
        greet(at(0, b, c))
    pl.when(not_first)(functools.partial(greet_x, -1))
    pl.when(not_last)(functools.partial(greet_x, 1))

    @pl.when(first)
    def _():
        for i in range(1, NX):
            greet((i, gy, gz))

    loads = [
        pltpu.make_async_copy(h, v, load_sem.at[i])
        for i, (h, v) in enumerate(
            ((stiff_h, stiff_v), (anchor_h, anchor_v), (adj_h, adj_v), (tile_h, tile_v),
             (row_h, row_v), (col_h, col_v), (off_h, off_v), (lin_h, lin_v))
        )
    ]
    for copy in loads:
        copy.start()

    lane = lax.broadcasted_iota(jnp.int32, (8, 128), 1)

    loads[0].wait()
    loads[1].wait()
    packed = jnp.zeros((8, 128), F32)
    for f, source in enumerate((stiff_v, anchor_v)):
        values = source[...].astype(F32)
        WX[f, 2:10, 0:8, 0:128] = values
        for z in range(BZ):
            w = f * BZ + z
            packed = jnp.where(lane // 8 == w, pltpu.roll(values[z], (8 * w + 4) % 128, 1), packed)
    PW[...] = packed

    loads[2].wait()
    packed = jnp.zeros((8, 128), F32)
    for v in range(VARIABLES):
        values = adj_v[v].astype(F32)
        AX[v, 0:8, 0:8, 0:128] = values
        for z in range(BZ):
            w = v * BZ + z
            packed = jnp.where(lane == w, pltpu.roll(values[z], w, 1), packed)
    PA[...] = packed

    for i in range(3, 7):
        loads[i].wait()
    TE[0, 0] = tile_v[...].astype(F32)
    TE[0, 1] = row_v[...].astype(F32)
    TE[0, 2] = col_v[...].astype(F32)
    TE[0, 3] = off_v[0]
    TE[0, 4] = off_v[1]

    pl.semaphore_wait(
        barrier,
        len(PLANE) + jnp.where(not_first, 10, 0) + jnp.where(not_last, 9, 0),
    )

    def w_copy(d):
        dx, dy, dz = d
        rs, rd = rows_between(dx)
        if dy == 0:
            zs, zd = layers_between(dz, 2, 1)
            src, dst = WX.at[:, pl.ds(2 + zs.start, zs.size), rs, 0:128], WX.at[:, zd, rs_at(rd), 0:128]
        else:
            src, dst = PW.at[rs], PWE.at[0 if dy == 1 else 1, 1 - dz, rd]
        i = near_index(d)
        return pltpu.make_async_remote_copy(
            src, dst, w_send.at[i], w_recv.at[i], device_id=at(*d), device_id_type=MESH
        )

    def rs_at(rd):
        return rd

    def a_copy(d):
        dx, dy, dz = d
        rs, rd = (pl.ds(0, 8), pl.ds(0, 8)) if dx == 0 else (pl.ds(0, 1), pl.ds(8, 1))
        if dy == 0:
            zs, zd = (pl.ds(0, 8), pl.ds(0, 8)) if dz == 0 else (pl.ds(0, 1), pl.ds(8, 1))
            src, dst = AX.at[:, zs, rs, 0:128], AX.at[:, zd, rd, 0:128]
        else:
            src, dst = PA.at[rs], PAE.at[-dz, rd]
        i = near_index(d)
        return pltpu.make_async_remote_copy(
            src, dst, a_send.at[i], a_recv.at[i], device_id=at(*d), device_id_type=MESH
        )

    def t_copy(a, b):
        i = 2 * a + b
        return pltpu.make_async_remote_copy(
            TE.at[0], TE.at[i], t_send.at[i], t_recv.at[i], device_id=at(a, b, 0), device_id_type=MESH
        )

    w_copies = [(d[0], w_copy(d)) for d in sorted(NEAR, key=lambda d: -sum(x >= 0 for x in d))]
    a_copies = [(d[0], a_copy(d)) for d in NEAR if max(d) <= 0]
    t_copies = [(a, t_copy(a, b)) for a, b in ((0, 1), (1, 0), (1, 1))]

    def start_all(copies):
        for step in (0, 1, -1):
            these = [c for dx, c in copies if dx == step]

            def go(these=these):
                for c in these:
                    c.start()

            guarded(can_send[step], go)

    def receive_all(copies):
        for step in (0, 1, -1):
            these = [c for dx, c in copies if dx == step]

            def go(these=these):
                for c in these:
                    c.wait_recv()

            guarded(can_receive[step], go)

    def sent_all(copies):
        for step in (0, 1, -1):
            these = [c for dx, c in copies if dx == step]

            def go(these=these):
                for c in these:
                    c.wait_send()

            guarded(can_send[step], go)

    start_all(w_copies)
    start_all(a_copies)
    start_all(t_copies)

    row16 = lax.broadcasted_iota(jnp.int32, (16, 256), 0)
    lane256 = lax.broadcasted_iota(jnp.int32, (16, 256), 1)
    ex = gx * BX + jnp.where(row16 < 12, row16, row16 - 16)
    ey = gy * BY + jnp.where(lane256 < 192, lane256, lane256 - 256)
    node_xy = (ex >= 0) & (ex <= NX * BX - 1) & (ey >= 0) & (ey <= NY * BY - 1)
    element_xy = (ex >= 0) & (ex <= NX * BX - 2) & (ey >= 0) & (ey <= NY * BY - 2)

    def node_mask(z):
        ez = gz * BZ + z
        return node_xy & (ez >= 0) & (ez <= NZ * BZ - 1)

    def element_mask(z):
        ez = gz * BZ + z
        return element_xy & (ez >= 0) & (ez <= NZ * BZ - 2)

    window16 = lax.broadcasted_iota(jnp.int32, (16, 128), 1)
    from_left = lax.rem(window16, 8) < 4

    receive_all(w_copies)
    for f in range(2):
        for z in range(-2, 9):
            slot, zz = (0, z + 8) if z < 0 else (1, z) if z < 8 else (2, z - 8)
            mixed = jnp.where(from_left, PWE[0, slot], PWE[1, slot])
            w = f * BZ + zz
            WX[f, z + 2, :, 128:256] = pltpu.roll(mixed, (124 - 8 * w) % 128, 1)
    for z in range(-2, 9):
        W16[z + 2] = jnp.where(element_mask(z), WX[0, z + 2], 0.0) * (1.0 / 16.0)
    highest = jnp.zeros((8, 128), F32)
    for z in range(-1, 9):
        total = W16[z + 1] + W16[z + 2]
        total = total + pltpu.roll(total, 1, 0)
        total = total + pltpu.roll(total, 1, 1)
        spring = jnp.where(node_mask(z), WX[1, z + 2], 0.0)
        DG[z + 1] = spring + 4.0 * total
        if 0 <= z < 8:
            highest = jnp.maximum(highest, (spring + 44.0 * total)[0:8, 0:128])

    P1[0:1] = jnp.max(highest, axis=0, keepdims=True)
    for b, c in PLANE:
        i = b * NZ + c
        pltpu.make_async_remote_copy(
            P1.at[pl.ds(0, 1)], P1.at[pl.ds(i, 1)], p1_send, p1_recv, device_id=at(0, b, c), device_id_type=MESH
        ).start()

    receive_all(a_copies)
    loads[7].wait()
    averages = []
    for v in range(VARIABLES):
        layers = []
        for z in range(BZ + 1):
            slot, zz = (0, z) if z < 8 else (1, 0)
            side = pltpu.roll(PAE[slot], (128 - (v * BZ + zz)) % 128, 1)
            layers.append(jnp.concatenate([AX[v, z, :, 0:128], side], axis=1))
        for z in range(BZ):
            total = layers[z] + layers[z + 1]
            total = total + pltpu.roll(total, 15, 0)
            total = total[0:8]
            total = total + pltpu.roll(total, 255, 1)
            AX[v, z, 0:8, 128:256] = total[:, 0:128] * (0.125 * 0.25)
    packs = [jnp.zeros((8, 128), F32), jnp.zeros((8, 128), F32)]
    for c in range(3):
        for z in range(BZ):
            total = lin_v[c, z].astype(F32) * AX[0, z, 0:8, 128:256]
            for v in range(1, VARIABLES):
                total = total + lin_v[3 * v + c, z].astype(F32) * AX[v, z, 0:8, 128:256]
            EX[c, z + 3, 0:8, 0:128] = total
            if z in EDGE_Z:
                t, w = 0, c * 5 + EDGE_Z.index(z)
            else:
                t, w = 1, c * 3 + INNER_Z.index(z)
            packs[t] = jnp.where(lane // 8 == w, pltpu.roll(total, (8 * w + 4) % 128, 1), packs[t])
    PS[0] = packs[0]
    PS[1] = packs[1]

    def s_copy(d):
        dx, dy, dz = d
        rs, rd = rows_between(dx)
        if dy == 0:
            zs, zd = layers_between(dz, 3, 2)
            src = EX.at[:, pl.ds(3 + zs.start, zs.size), rs, 0:128]
            dst = EX.at[:, zd, rd, 0:128]
        else:
            side = 0 if dy == 1 else 1
            if dz == 0:
                src, dst = PS.at[:, rs], PSE.at[side, pl.ds(1, 2), rd]
            else:
                src, dst = PS.at[0, rs], PSE.at[side, 0 if dz == 1 else 3, rd]
        i = near_index(d)
        return pltpu.make_async_remote_copy(
            src, dst, s_send.at[i], s_recv.at[i], device_id=at(*d), device_id_type=MESH
        )

    s_copies = [(d[0], s_copy(d)) for d in sorted(NEAR, key=lambda d: abs(d[1]))]
    start_all(s_copies)

    receive_all(t_copies)
    mine = (gx * NY + gy).astype(F32)
    rows = lax.broadcasted_iota(jnp.int32, (256, 128), 0).astype(F32)
    columns = lax.broadcasted_iota(jnp.int32, (128, 128), 0).astype(F32)
    for q in range(4):
        here = TE[q, 0] == mine
        if q >= 2:
            here = here & not_first
        row_at = jnp.where(here, TE[q, 1], -9.0)
        col_at = jnp.where(here, TE[q, 2], -9.0)
        fr = jnp.where(here, TE[q, 3], 0.0)
        fc = jnp.where(here, TE[q, 4], 0.0)
        for x in range(BX):
            part = pl.ds((q * BX + x) * 128, 128)
            r, f = row_at[x : x + 1], fr[x : x + 1]
            value = jnp.where(rows == r, 1.0 - f, jnp.where(rows == r + 1.0, f, 0.0))
            high = value.astype(BF16)
            RH[:, part] = high
            RL[:, part] = (value - high.astype(F32)).astype(BF16)
            r, f = col_at[x : x + 1], fc[x : x + 1]
            CV[:, part] = jnp.where(columns == r, 1.0 - f, jnp.where(columns == r + 1.0, f, 0.0))

    pltpu.make_async_copy(P1.at[pl.ds(1, 31)], P1.at[pl.ds(1, 31)], p1_recv).wait()
    plane_highest = jnp.max(P1[...], axis=0, keepdims=True)
    P2[0:1] = plane_highest
    up = pltpu.make_async_remote_copy(
        P2.at[pl.ds(0, 1)], P2.at[pl.ds(gx, 1)], p2_send, p2_recv, device_id=(0, gy, gz), device_id_type=MESH
    )
    pl.when(not_first)(up.start)

    receive_all(s_copies)
    for side_slot in range(1):
        mixed = [jnp.where(from_left, PSE[0, s], PSE[1, s]) for s in range(4)]
        for c in range(3):
            for z in range(-3, 10):
                zz = z % 8
                if zz in EDGE_Z:
                    slot, w = (0 if z < 0 else 3 if z >= 8 else 1), c * 5 + EDGE_Z.index(zz)
                else:
                    slot, w = 2, c * 3 + INNER_Z.index(zz)
                EX[c, z + 3, :, 128:256] = pltpu.roll(mixed[slot], (124 - 8 * w) % 128, 1)

    def ahead_x(value):
        return pltpu.roll(value, 15, 0)

    def ahead_y(value):
        return pltpu.roll(value, 255, 1)

    def behind_x(value):
        return pltpu.roll(value, 1, 0)

    def behind_y(value):
        return pltpu.roll(value, 1, 1)

    held = None
    for z in range(-3, 10):
        mask = element_mask(z)
        sense = [jnp.where(mask, EX[c, z + 3], 0.0) for c in range(3)]
        if held is not None:
            qx, qy, qz = held[0] + sense[0], held[1] + sense[1], held[2] - sense[2]
            qx, qy, qz = behind_x(qx) - qx, behind_x(qy) + qy, behind_x(qz) + qz
            G[0, z + 2] = behind_y(qx) + qx
            G[1, z + 2] = behind_y(qy) - qy
            G[2, z + 2] = behind_y(qz) + qz
        held = sense

    def element_forces(low, high, weight):
        gradient, middle = [], []
        for c in range(3):
            a, b = high[c] + low[c], high[c] - low[c]
            a1, b1 = ahead_y(a), ahead_y(b)
            sy, dy, sz = a1 + a, a1 - a, b1 + b
            sy1, dy1, sz1 = ahead_x(sy), ahead_x(dy), ahead_x(sz)
            middle.append(sy1 + sy)
            gradient.append((sy1 - sy, dy1 + dy, sz1 + sz))
        trace = gradient[0][0] + gradient[1][1] + gradient[2][2]
        half = 0.5 * weight
        plus, minus = [], []
        for c in range(3):
            s = [
                weight * (2.0 * gradient[c][c] + trace if c == d else gradient[c][d] + gradient[d][c])
                for d in range(3)
            ]
            m = half * middle[c]
            q = behind_x(s[0] - m) - (s[0] + m)
            q2 = behind_x(s[1]) + s[1]
            q3 = behind_x(s[2]) + s[2]
            r1 = behind_y(q + q2) + (q - q2)
            r2 = behind_y(q3) + q3
            plus.append(r1 + r2)
            minus.append(r1 - r2)
        return plus, minus

    held = None
    for j in range(11):
        plus, minus = element_forces([G[c, j] for c in range(3)], [G[c, j + 1] for c in range(3)], W16[j])
        if held is not None:
            for c in range(3):
                K1[c, j - 1] = held[c] + minus[c] + DG[j - 1] * G[c, j]
        held = plus

    sums = [jnp.zeros((8, 128), F32) for _ in range(3)]
    held = None
    for j in range(9):
        plus, minus = element_forces([K1[c, j] for c in range(3)], [K1[c, j + 1] for c in range(3)], W16[j + 1])
        if held is not None:
            z = j - 1
            for c in range(3):
                value = held[c] + minus[c] + DG[j] * K1[c, j]
                K2[c, z] = value[0:8, 0:128]
            share = ((NZ * BZ - 1 - z) - gz * BZ).astype(F32) * (1.0 / (NZ * BZ - 1))
            sums[0] = sums[0] + share * G[2, z + 2, 0:8, 0:128]
            sums[1] = sums[1] + share * K1[2, z + 1, 0:8, 0:128]
            sums[2] = sums[2] + share * K2[2, z]
        held = plus
    for k in range(3):
        CE[0, k] = sums[k]

    def e_copy(a, b, c):
        i = a * 8 + b * 4 + c
        return pltpu.make_async_remote_copy(
            CE.at[0], CE.at[i], e_send.at[a], e_recv.at[a], device_id=at(a, b, c), device_id_type=MESH
        )

    for a in (0, 1):
        these = [e_copy(*d) for d in GROUND if d[0] == a and d != (0, 0, 0)]

        def go(these=these):
            for copy in these:
                copy.start()

        guarded(can_send[a], go)

    @pl.when(first)
    def _():
        pltpu.make_async_copy(P2.at[pl.ds(1, 15)], P2.at[pl.ds(1, 15)], p2_recv).wait()
        P3[...] = jnp.max(P2[...], axis=0, keepdims=True)
        for i in range(1, NX):
            pltpu.make_async_remote_copy(
                P3, P3, p3_send, p3_recv, device_id=(i, gy, gz), device_id_type=MESH
            ).start()

    @pl.when(not_first)
    def _():
        pltpu.make_async_copy(P3, P3, p3_recv).wait()

    top = jnp.max(P3[...], axis=1, keepdims=True)
    low = top / 30.0
    center = 0.5 * (top + low)
    half_width = 0.5 * (top - low)
    ratio = center / half_width
    rho0 = 1.0 / ratio
    rho1 = 1.0 / (2.0 * ratio - rho0)
    rho2 = 1.0 / (2.0 * ratio - rho1)
    inverse = 1.0 / center
    a1, b1 = rho1 * rho0, 2.0 * rho1 / half_width
    a2, b2 = rho2 * rho1, 2.0 * rho2 / half_width
    p, q = a1 * inverse + b1, -b1 * inverse
    k0 = inverse + p + a2 * p + b2
    k1 = q + a2 * q - b2 * (inverse + p)
    k2 = -b2 * q
    k0, k1, k2 = [jnp.broadcast_to(k, (8, 128)) for k in (k0, k1, k2)]
    for c in range(3):
        for z in range(BZ):
            def_o[c, z] = k0 * G[c, z + 2, 0:8, 0:128] + k1 * K1[c, z + 1, 0:8, 0:128] + k2 * K2[c, z]

    pltpu.make_async_copy(CE.at[pl.ds(1, 7)], CE.at[pl.ds(1, 7)], e_recv.at[0]).wait()

    @pl.when(not_first)
    def _():
        pltpu.make_async_copy(CE.at[pl.ds(8, 8)], CE.at[pl.ds(8, 8)], e_recv.at[1]).wait()

    result = jnp.zeros((256, 128), F32)
    for q in range(4):
        parts = [
            CE[4 * q, k] + CE[4 * q + 1, k] + CE[4 * q + 2, k] + CE[4 * q + 3, k] for k in range(3)
        ]
        column = k0 * parts[0] + k1 * parts[1] + k2 * parts[2]
        if q >= 2:
            column = jnp.where(not_first, column, 0.0)
        for x in range(BX):
            part = pl.ds((q * BX + x) * 128, 128)
            value = CV[:, part] * column[x : x + 1]
            high = value.astype(BF16)
            rest = (value - high.astype(F32)).astype(BF16)
            both = jnp.concatenate([high, rest], axis=0)
            dims = (((1,), (1,)), ((), ()))
            pair = lax.dot_general(RH[:, part], both, dims, preferred_element_type=F32)
            result = result + pair[:, 0:128] + pair[:, 128:256]
            result = result + lax.dot_general(RL[:, part], high, dims, preferred_element_type=F32)
    dem_o[...] = result

    sent_all(w_copies)
    sent_all(a_copies)
    sent_all(t_copies)
    sent_all(s_copies)
    pltpu.make_async_copy(P1.at[pl.ds(1, 31)], P1.at[pl.ds(1, 31)], p1_send).wait()
    pl.when(not_first)(up.wait_send)
    pltpu.make_async_copy(CE.at[pl.ds(1, 7)], CE.at[pl.ds(1, 7)], e_send.at[0]).wait()

    @pl.when(not_last)
    def _():
        pltpu.make_async_copy(CE.at[pl.ds(8, 8)], CE.at[pl.ds(8, 8)], e_send.at[1]).wait()

    @pl.when(first)
    def _():
        pltpu.make_async_copy(P2.at[pl.ds(1, 15)], P2.at[pl.ds(1, 15)], p3_send).wait()


def per_device(adjoint, linearized, stiffness, anchor, target_tile, target_row, target_col, offsets):
    vmem = lambda *shape, dtype=F32: pltpu.VMEM(shape, dtype)
    dma = pltpu.SemaphoreType.DMA
    ground = (BX, BY)
    return pl.pallas_call(
        kernel,
        out_shape=(
            jax.ShapeDtypeStruct((3, BZ, BX, BY), F32),
            jax.ShapeDtypeStruct((TILE_ROWS, TILE_COLUMNS), F32),
        ),
        in_specs=[pl.BlockSpec(memory_space=pl.ANY)] * 8,
        out_specs=[pl.BlockSpec(memory_space=pltpu.VMEM)] * 2,
        scratch_shapes=[
            vmem(6, BZ, BX, BY, dtype=BF16), vmem(18, BZ, BX, BY, dtype=BF16),
            vmem(BZ, BX, BY, dtype=BF16), vmem(BZ, BX, BY),
            vmem(*ground, dtype=jnp.int32), vmem(*ground, dtype=jnp.int32),
            vmem(*ground, dtype=jnp.int32), vmem(2, *ground),
            vmem(VARIABLES, AZ, 16, 256), vmem(8, 128), vmem(2, 16, 128),
            vmem(2, WZ, 16, 256), vmem(8, 128), vmem(2, 3, 16, 128),
            vmem(3, SZ, 16, 256), vmem(2, 8, 128), vmem(2, 4, 16, 128),
            vmem(4, 5, 8, 128),
            vmem(WZ, 16, 256), vmem(10, 16, 256),
            vmem(3, 12, 16, 256), vmem(3, 10, 16, 256), vmem(3, BZ, BX, BY),
            vmem(16, 3, 8, 128), vmem(32, 128), vmem(16, 128), vmem(1, 128),
            vmem(256, 4096, dtype=BF16), vmem(256, 4096, dtype=BF16), vmem(128, 4096),
            dma((8,)), dma((27,)), dma((27,)), dma((27,)), dma((27,)), dma((4,)), dma((4,)),
            dma((27,)), dma((27,)), dma((2,)), dma((2,)), dma, dma, dma, dma, dma, dma,
        ],
        compiler_params=pltpu.CompilerParams(
            collective_id=0, has_side_effects=True, vmem_limit_bytes=48 * 1024 * 1024
        ),
    )(
        adjoint, linearized, stiffness, anchor,
        target_tile.reshape(ground), target_row.reshape(ground), target_col.reshape(ground),
        offsets.reshape((2,) + ground),
    )


def solution(mesh):
    in_specs = (
        P(None, "gz", "gx", "gy"),
        P(None, "gz", "gx", "gy"),
        P("gz", "gx", "gy"),
        P("gz", "gx", "gy"),
        P("gx", "gy", None, None),
        P("gx", "gy", None),
        P("gx", "gy", None),
        P(None, "gx", "gy", None),
    )
    out_specs = (P(None, "gz", "gx", "gy"), P("gy", "gx"))
    return jax.shard_map(per_device, mesh=mesh, in_specs=in_specs, out_specs=out_specs, check_vma=False)
```

```python
import functools
import itertools

import jax
import jax.numpy as jnp
from jax import lax
from jax.experimental import pallas as pl
from jax.experimental.pallas import tpu as pltpu
from jax.sharding import PartitionSpec as P

MESH = pl.DeviceIdType.MESH
F32, BF16 = jnp.float32, jnp.bfloat16
NX, NY, NZ = 16, 8, 4
BZ, BX, BY = 8, 8, 128
TILE_ROWS, TILE_COLUMNS = 256, 128
VARIABLES = 6
SZ, WZ, AZ = 13, 11, 9
EDGE_Z, INNER_Z = (5, 6, 7, 0, 1), (2, 3, 4)

NEAR = [d for d in itertools.product((-1, 0, 1), repeat=3) if d != (0, 0, 0)]
PLANE = sorted(
    [(b, c) for b in range(NY) for c in range(NZ) if (b, c) != (0, 0)],
    key=lambda d: -(min(d[0], NY - d[0]) // 2 + min(d[1], NZ - d[1])),
)
DOWN = [d for d in NEAR if max(d) <= 0]
UP = [d for d in NEAR if min(d) >= 0]
SIDES = [d for d in NEAR if max(d) > 0]
ROOTS = 4
GROUND = [(a, b, c) for a in (0, 1) for b in (0, 1) for c in range(NZ)]


def near_index(d):
    return (d[0] + 1) * 9 + (d[1] + 1) * 3 + d[2] + 1


def guarded(condition, act):
    if condition is None:
        act()
    else:
        pl.when(condition)(act)


def rows_between(dx):
    if dx == 0:
        return pl.ds(0, 8), pl.ds(0, 8)
    return (pl.ds(4, 4), pl.ds(12, 4)) if dx == 1 else (pl.ds(0, 4), pl.ds(8, 4))


def layers_between(dz, below, above):
    if dz == 0:
        return pl.ds(0, BZ), pl.ds(below, BZ)
    if dz == 1:
        return pl.ds(BZ - below, below), pl.ds(0, below)
    return pl.ds(0, above), pl.ds(below + BZ, above)


def kernel(
    adj_h, lin_h, stiff_h, anchor_h, tile_h, row_h, col_h, off_h,
    parts_o, tiles_o, peak_o,
    adj_v, lin_v, stiff_v, anchor_v, tile_v, row_v, col_v, off_v,
    AX, PA, PAE, WX, PW, PWE, EX, PS, PSE, TE, W16, DG, G, K1, CE, P1, P2, P3,
    RH, RL, CV, CH, CL,
    load_sem, w_send, w_recv, a_send, a_recv, t_send, t_recv, s_send, s_recv,
    e_send, e_recv, p1_send, p1_recv, p2_send, p2_recv, p3_send, p3_recv,
):
    gx, gy, gz = lax.axis_index("gx"), lax.axis_index("gy"), lax.axis_index("gz")

    def at(dx, dy, dz):
        return (gx + dx, lax.rem(gy + dy + NY, NY), lax.rem(gz + dz + NZ, NZ))

    not_first, not_last, is_root = gx > 0, gx < NX - 1, gx < ROOTS
    can_send = {0: None, 1: not_last, -1: not_first}
    can_receive = {0: None, 1: not_first, -1: not_last}

    barrier = pltpu.get_barrier_semaphore()

    def greet(device):
        pl.semaphore_signal(barrier, inc=1, device_id=device, device_id_type=MESH)

    def greet_near(steps):
        for dx in (0, 1, -1):
            these = [d for d in steps if d[0] == dx]

            def go(these=these):
                for d in these:
                    greet(at(*d))

            guarded(can_send[dx], go)

    greet_near(DOWN)
    greet_near(SIDES)
    for b, c in PLANE:
        if (0, (b + 1) % NY - 1, (c + 1) % NZ - 1) not in NEAR:
            greet(at(0, b, c))

    @pl.when(is_root)
    def _():
        for i in range(1, NX):
            greet((lax.rem(gx + i, NX), gy, gz))

    loads = [
        pltpu.make_async_copy(h, v, load_sem.at[i])
        for i, (h, v) in enumerate(
            ((stiff_h, stiff_v), (anchor_h, anchor_v), (adj_h, adj_v), (tile_h, tile_v),
             (row_h, row_v), (col_h, col_v), (off_h, off_v), (lin_h, lin_v))
        )
    ]
    for copy in loads:
        copy.start()

    lane = lax.broadcasted_iota(jnp.int32, (8, 128), 1)

    loads[0].wait()
    loads[1].wait()
    packed = jnp.zeros((8, 128), F32)
    for f, source in enumerate((stiff_v, anchor_v)):
        values = source[...].astype(F32)
        WX[f, 2:10, 0:8, 0:128] = values
        for z in range(BZ):
            w = f * BZ + z
            packed = jnp.where(lane // 8 == w, pltpu.roll(values[z], (8 * w + 4) % 128, 1), packed)
    PW[...] = packed

    loads[2].wait()
    packed = jnp.zeros((8, 128), F32)
    for v in range(VARIABLES):
        values = adj_v[v].astype(F32)
        AX[v, 0:8, 0:8, 0:128] = values
        for z in range(BZ):
            w = v * BZ + z
            packed = jnp.where(lane == w, pltpu.roll(values[z], w, 1), packed)
    PA[...] = packed

    for i in range(3, 7):
        loads[i].wait()
    TE[0, 0] = tile_v[...].astype(F32)
    TE[0, 1] = row_v[...].astype(F32)
    TE[0, 2] = col_v[...].astype(F32)
    TE[0, 3] = off_v[0]
    TE[0, 4] = off_v[1]

    pl.semaphore_wait(
        barrier,
        len(PLANE) + jnp.where(not_first, 9, 0) + jnp.where(not_last, 9, 0) + jnp.where(is_root, ROOTS - 1, ROOTS),
    )

    def w_copy(d):
        dx, dy, dz = d
        rs, rd = rows_between(dx)
        if dy == 0:
            zs, zd = layers_between(dz, 2, 1)
            src, dst = WX.at[:, pl.ds(2 + zs.start, zs.size), rs, 0:128], WX.at[:, zd, rs_at(rd), 0:128]
        else:
            src, dst = PW.at[rs], PWE.at[0 if dy == 1 else 1, 1 - dz, rd]
        i = near_index(d)
        return pltpu.make_async_remote_copy(
            src, dst, w_send.at[i], w_recv.at[i], device_id=at(*d), device_id_type=MESH
        )

    def rs_at(rd):
        return rd

    def a_copy(d):
        dx, dy, dz = d
        rs, rd = (pl.ds(0, 8), pl.ds(0, 8)) if dx == 0 else (pl.ds(0, 1), pl.ds(8, 1))
        if dy == 0:
            zs, zd = (pl.ds(0, 8), pl.ds(0, 8)) if dz == 0 else (pl.ds(0, 1), pl.ds(8, 1))
            src, dst = AX.at[:, zs, rs, 0:128], AX.at[:, zd, rd, 0:128]
        else:
            src, dst = PA.at[rs], PAE.at[-dz, rd]
        i = near_index(d)
        return pltpu.make_async_remote_copy(
            src, dst, a_send.at[i], a_recv.at[i], device_id=at(*d), device_id_type=MESH
        )

    def t_copy(a, b):
        i = 2 * a + b
        return pltpu.make_async_remote_copy(
            TE.at[0], TE.at[i], t_send.at[i], t_recv.at[i], device_id=at(a, b, 0), device_id_type=MESH
        )

    w_up = [(d[0], w_copy(d)) for d in UP]
    w_rest = [(d[0], w_copy(d)) for d in NEAR if d not in UP]
    a_copies = [(d[0], a_copy(d)) for d in DOWN]
    t_copies = [(a, t_copy(a, b)) for a, b in ((0, 1), (1, 0), (1, 1))]

    def start_all(copies):
        for step in (0, 1, -1):
            these = [c for dx, c in copies if dx == step]

            def go(these=these):
                for c in these:
                    c.start()

            guarded(can_send[step], go)

    def receive_all(copies):
        for step in (0, 1, -1):
            these = [c for dx, c in copies if dx == step]

            def go(these=these):
                for c in these:
                    c.wait_recv()

            guarded(can_receive[step], go)

    def sent_all(copies):
        for step in (0, 1, -1):
            these = [c for dx, c in copies if dx == step]

            def go(these=these):
                for c in these:
                    c.wait_send()

            guarded(can_send[step], go)

    start_all(w_up)
    start_all(a_copies)
    start_all(w_rest)
    start_all(t_copies)

    row16 = lax.broadcasted_iota(jnp.int32, (16, 256), 0)
    lane256 = lax.broadcasted_iota(jnp.int32, (16, 256), 1)
    ex = gx * BX + jnp.where(row16 < 12, row16, row16 - 16)
    ey = gy * BY + jnp.where(lane256 < 192, lane256, lane256 - 256)
    node_xy = (ex >= 0) & (ex <= NX * BX - 1) & (ey >= 0) & (ey <= NY * BY - 1)
    element_xy = (ex >= 0) & (ex <= NX * BX - 2) & (ey >= 0) & (ey <= NY * BY - 2)

    def node_mask(z):
        ez = gz * BZ + z
        return node_xy & (ez >= 0) & (ez <= NZ * BZ - 1)

    def element_mask(z):
        ez = gz * BZ + z
        return element_xy & (ez >= 0) & (ez <= NZ * BZ - 2)

    window16 = lax.broadcasted_iota(jnp.int32, (16, 128), 1)
    from_left = lax.rem(window16, 8) < 4

    receive_all(w_up)
    row8 = lax.broadcasted_iota(jnp.int32, (8, 128), 0)
    here_x, here_y = gx * BX + row8 <= NX * BX - 2, gy * BY + lane <= NY * BY - 2
    held, highest = None, jnp.zeros((8, 128), F32)
    for z in range(-1, BZ):
        slot, zz = (0, z + 8) if z < 0 else (1, z)
        shift = (124 - 8 * zz) % 128
        there = (gz * BZ + z >= 0) & (gz * BZ + z <= NZ * BZ - 2)
        main = jnp.where(here_x & here_y & there, WX[0, z + 2, 0:8, 0:128], 0.0)
        side = jnp.where(here_x & (gy > 0) & there, pltpu.roll(PWE[0, slot, 0:8], shift, 1), 0.0)
        under = jnp.where(here_y[0:1] & not_first & there, WX[0, z + 2, 12:16, 0:128][3:4], 0.0)
        corner = jnp.where(not_first & (gy > 0) & there, pltpu.roll(PWE[0, slot, 12:16], shift, 1)[3:4], 0.0)
        main = main + jnp.where(row8 == 0, under, pltpu.roll(main, 1, 0))
        side = side + jnp.where(row8 == 0, corner, pltpu.roll(side, 1, 0))
        layer = main + jnp.where(lane == 0, pltpu.roll(side, 1, 1), pltpu.roll(main, 1, 1))
        if held is not None:
            highest = jnp.maximum(highest, anchor_v[z] + 2.75 * (held + layer))
        held = layer

    P1[0:1] = jnp.max(highest, axis=0, keepdims=True)
    for b, c in PLANE:
        i = b * NZ + c
        pltpu.make_async_remote_copy(
            P1.at[pl.ds(0, 1)], P1.at[pl.ds(i, 1)], p1_send, p1_recv, device_id=at(0, b, c), device_id_type=MESH
        ).start()

    receive_all(a_copies)
    loads[7].wait()
    averages = []
    for v in range(VARIABLES):
        layers = []
        for z in range(BZ + 1):
            slot, zz = (0, z) if z < 8 else (1, 0)
            side = pltpu.roll(PAE[slot], (128 - (v * BZ + zz)) % 128, 1)
            layers.append(jnp.concatenate([AX[v, z, :, 0:128], side], axis=1))
        for z in range(BZ):
            total = layers[z] + layers[z + 1]
            total = total + pltpu.roll(total, 15, 0)
            total = total[0:8]
            total = total + pltpu.roll(total, 255, 1)
            AX[v, z, 0:8, 128:256] = total[:, 0:128] * (0.125 * 0.25)
    packs = [jnp.zeros((8, 128), F32), jnp.zeros((8, 128), F32)]
    for c in range(3):
        for z in range(BZ):
            total = lin_v[c, z].astype(F32) * AX[0, z, 0:8, 128:256]
            for v in range(1, VARIABLES):
                total = total + lin_v[3 * v + c, z].astype(F32) * AX[v, z, 0:8, 128:256]
            EX[c, z + 3, 0:8, 0:128] = total
            if z in EDGE_Z:
                t, w = 0, c * 5 + EDGE_Z.index(z)
            else:
                t, w = 1, c * 3 + INNER_Z.index(z)
            packs[t] = jnp.where(lane // 8 == w, pltpu.roll(total, (8 * w + 4) % 128, 1), packs[t])
    PS[0] = packs[0]
    PS[1] = packs[1]

    def s_copy(d):
        dx, dy, dz = d
        rs, rd = rows_between(dx)
        if dy == 0:
            zs, zd = layers_between(dz, 3, 2)
            src = EX.at[:, pl.ds(3 + zs.start, zs.size), rs, 0:128]
            dst = EX.at[:, zd, rd, 0:128]
        else:
            side = 0 if dy == 1 else 1
            if dz == 0:
                src, dst = PS.at[:, rs], PSE.at[side, pl.ds(1, 2), rd]
            else:
                src, dst = PS.at[0, rs], PSE.at[side, 0 if dz == 1 else 3, rd]
        i = near_index(d)
        return pltpu.make_async_remote_copy(
            src, dst, s_send.at[i], s_recv.at[i], device_id=at(*d), device_id_type=MESH
        )

    s_copies = [(d[0], s_copy(d)) for d in sorted(NEAR, key=lambda d: abs(d[1]))]
    start_all(s_copies)

    pltpu.make_async_copy(P1.at[pl.ds(1, 31)], P1.at[pl.ds(1, 31)], p1_recv).wait()
    P2[pl.ds(gx, 1)] = jnp.max(P1[...], axis=0, keepdims=True)
    own = pl.ds(gx, 1)
    ups = [
        pltpu.make_async_remote_copy(
            P2.at[own], P2.at[own], p2_send, p2_recv, device_id=(r, gy, gz), device_id_type=MESH
        )
        for r in range(ROOTS)
    ]
    for r in range(ROOTS):
        pl.when(gx != r)(ups[r].start)

    receive_all(w_rest)
    for f in range(2):
        for z in range(-2, 9):
            slot, zz = (0, z + 8) if z < 0 else (1, z) if z < 8 else (2, z - 8)
            mixed = jnp.where(from_left, PWE[0, slot], PWE[1, slot])
            w = f * BZ + zz
            WX[f, z + 2, :, 128:256] = pltpu.roll(mixed, (124 - 8 * w) % 128, 1)
    for z in range(-2, 9):
        W16[z + 2] = jnp.where(element_mask(z), WX[0, z + 2], 0.0) * (1.0 / 16.0)
    for z in range(-1, 9):
        total = W16[z + 1] + W16[z + 2]
        total = total + pltpu.roll(total, 1, 0)
        total = total + pltpu.roll(total, 1, 1)
        spring = jnp.where(node_mask(z), WX[1, z + 2], 0.0)
        DG[z + 1] = spring + 4.0 * total

    receive_all(t_copies)
    mine = (gx * NY + gy).astype(F32)
    rows = lax.broadcasted_iota(jnp.int32, (256, 128), 0).astype(F32)
    columns = lax.broadcasted_iota(jnp.int32, (128, 128), 0).astype(F32)
    for q in range(4):
        here = TE[q, 0] == mine
        if q >= 2:
            here = here & not_first
        row_at = jnp.where(here, TE[q, 1], -9.0)
        col_at = jnp.where(here, TE[q, 2], -9.0)
        fr = jnp.where(here, TE[q, 3], 0.0)
        fc = jnp.where(here, TE[q, 4], 0.0)
        for x in range(BX):
            part = pl.ds((q * BX + x) * 128, 128)
            r, f = row_at[x : x + 1], fr[x : x + 1]
            value = jnp.where(rows == r, 1.0 - f, jnp.where(rows == r + 1.0, f, 0.0))
            high = value.astype(BF16)
            RH[:, part] = high
            RL[:, part] = (value - high.astype(F32)).astype(BF16)
            r, f = col_at[x : x + 1], fc[x : x + 1]
            CV[:, part] = jnp.where(columns == r, 1.0 - f, jnp.where(columns == r + 1.0, f, 0.0))

    receive_all(s_copies)
    for side_slot in range(1):
        mixed = [jnp.where(from_left, PSE[0, s], PSE[1, s]) for s in range(4)]
        for c in range(3):
            for z in range(-3, 10):
                zz = z % 8
                if zz in EDGE_Z:
                    slot, w = (0 if z < 0 else 3 if z >= 8 else 1), c * 5 + EDGE_Z.index(zz)
                else:
                    slot, w = 2, c * 3 + INNER_Z.index(zz)
                EX[c, z + 3, :, 128:256] = pltpu.roll(mixed[slot], (124 - 8 * w) % 128, 1)

    def ahead_x(value):
        return pltpu.roll(value, 15, 0)

    def ahead_y(value):
        return pltpu.roll(value, 255, 1)

    def behind_x(value):
        return pltpu.roll(value, 1, 0)

    def behind_y(value):
        return pltpu.roll(value, 1, 1)

    held = None
    for z in range(-3, 10):
        mask = element_mask(z)
        sense = [jnp.where(mask, EX[c, z + 3], 0.0) for c in range(3)]
        if held is not None:
            qx, qy, qz = held[0] + sense[0], held[1] + sense[1], held[2] - sense[2]
            qx, qy, qz = behind_x(qx) - qx, behind_x(qy) + qy, behind_x(qz) + qz
            G[0, z + 2] = behind_y(qx) + qx
            G[1, z + 2] = behind_y(qy) - qy
            G[2, z + 2] = behind_y(qz) + qz
            if 0 <= z < BZ:
                for c in range(3):
                    parts_o[0, c, z] = G[c, z + 2, 0:8, 0:128]
        held = sense

    def element_forces(low, high, weight):
        gradient, middle = [], []
        for c in range(3):
            a, b = high[c] + low[c], high[c] - low[c]
            a1, b1 = ahead_y(a), ahead_y(b)
            sy, dy, sz = a1 + a, a1 - a, b1 + b
            sy1, dy1, sz1 = ahead_x(sy), ahead_x(dy), ahead_x(sz)
            middle.append(sy1 + sy)
            gradient.append((sy1 - sy, dy1 + dy, sz1 + sz))
        trace = gradient[0][0] + gradient[1][1] + gradient[2][2]
        half = 0.5 * weight
        plus, minus = [], []
        for c in range(3):
            s = [
                weight * (2.0 * gradient[c][c] + trace if c == d else gradient[c][d] + gradient[d][c])
                for d in range(3)
            ]
            m = half * middle[c]
            q = behind_x(s[0] - m) - (s[0] + m)
            q2 = behind_x(s[1]) + s[1]
            q3 = behind_x(s[2]) + s[2]
            r1 = behind_y(q + q2) + (q - q2)
            r2 = behind_y(q3) + q3
            plus.append(r1 + r2)
            minus.append(r1 - r2)
        return plus, minus

    held = None
    for j in range(11):
        plus, minus = element_forces([G[c, j] for c in range(3)], [G[c, j + 1] for c in range(3)], W16[j])
        if held is not None:
            for c in range(3):
                value = held[c] + minus[c] + DG[j - 1] * G[c, j]
                K1[c, j - 1] = value
                if 0 <= j - 2 < BZ:
                    parts_o[1, c, j - 2] = value[0:8, 0:128]
        held = plus

    sums = [jnp.zeros((8, 128), F32) for _ in range(3)]
    held = None
    for j in range(9):
        plus, minus = element_forces([K1[c, j] for c in range(3)], [K1[c, j + 1] for c in range(3)], W16[j + 1])
        if held is not None:
            z = j - 1
            for c in range(3):
                value = held[c] + minus[c] + DG[j] * K1[c, j]
                parts_o[2, c, z] = value[0:8, 0:128]
            share = ((NZ * BZ - 1 - z) - gz * BZ).astype(F32) * (1.0 / (NZ * BZ - 1))
            for k in range(3):
                sums[k] = sums[k] + share * parts_o[k, 2, z]
        held = plus
    for k in range(3):
        CE[0, k] = sums[k]

    def e_copy(a, b, c):
        i = a * 8 + b * 4 + c
        return pltpu.make_async_remote_copy(
            CE.at[0], CE.at[i], e_send.at[a], e_recv.at[a], device_id=at(a, b, c), device_id_type=MESH
        )

    for a in (0, 1):
        these = [e_copy(*d) for d in GROUND if d[0] == a and d != (0, 0, 0)]

        def go(these=these):
            for copy in these:
                copy.start()

        guarded(can_send[a], go)

    pltpu.make_async_copy(CE.at[pl.ds(1, 7)], CE.at[pl.ds(1, 7)], e_recv.at[0]).wait()

    @pl.when(not_first)
    def _():
        pltpu.make_async_copy(CE.at[pl.ds(8, 8)], CE.at[pl.ds(8, 8)], e_recv.at[1]).wait()

    for q in range(4):
        columns = [CE[4 * q, k] + CE[4 * q + 1, k] + CE[4 * q + 2, k] + CE[4 * q + 3, k] for k in range(3)]
        if q >= 2:
            columns = [jnp.where(not_first, column, 0.0) for column in columns]
        for x in range(BX):
            part = pl.ds((q * BX + x) * 128, 128)
            for k in range(3):
                value = CV[:, part] * columns[k][x : x + 1]
                high = value.astype(BF16)
                CH[k * 128 : k * 128 + 128, part] = high
                CL[k * 128 : k * 128 + 128, part] = (value - high.astype(F32)).astype(BF16)
    dims = (((1,), (1,)), ((), ()))

    def times(a, b):
        return lax.dot_general(a, b, dims, preferred_element_type=F32)

    tiles = times(RH[...], CH[...]) + times(RH[...], CL[...]) + times(RL[...], CH[...])
    for k in range(3):
        tiles_o[k] = tiles[:, k * 128 : k * 128 + 128]

    @pl.when(is_root)
    def _():
        pltpu.make_async_copy(P2.at[pl.ds(1, 15)], P2.at[pl.ds(1, 15)], p2_recv).wait()
        P3[...] = jnp.max(P2[...], axis=0, keepdims=True)
        for i in range(3):
            pltpu.make_async_remote_copy(
                P3, P3, p3_send, p3_recv, device_id=(13 - 3 * gx + i, gy, gz), device_id_type=MESH
            ).start()

    @pl.when(jnp.logical_not(is_root))
    def _():
        pltpu.make_async_copy(P3, P3, p3_recv).wait()

    peak_o[...] = jnp.broadcast_to(P3[...], (8, 128))

    sent_all(w_up)
    sent_all(w_rest)
    sent_all(a_copies)
    sent_all(t_copies)
    sent_all(s_copies)
    pltpu.make_async_copy(P1.at[pl.ds(1, 31)], P1.at[pl.ds(1, 31)], p1_send).wait()
    for r in range(ROOTS):
        pl.when(gx != r)(ups[r].wait_send)
    pltpu.make_async_copy(CE.at[pl.ds(1, 7)], CE.at[pl.ds(1, 7)], e_send.at[0]).wait()

    @pl.when(not_last)
    def _():
        pltpu.make_async_copy(CE.at[pl.ds(8, 8)], CE.at[pl.ds(8, 8)], e_send.at[1]).wait()

    @pl.when(is_root)
    def _():
        pltpu.make_async_copy(P2.at[pl.ds(1, 3)], P2.at[pl.ds(1, 3)], p3_send).wait()


def combine(parts, tiles, peak, def_o, dem_o):
    top = jnp.max(peak[...], axis=1, keepdims=True)
    low = top / 30.0
    center = 0.5 * (top + low)
    half_width = 0.5 * (top - low)
    ratio = center / half_width
    rho0 = 1.0 / ratio
    rho1 = 1.0 / (2.0 * ratio - rho0)
    rho2 = 1.0 / (2.0 * ratio - rho1)
    inverse = 1.0 / center
    a1, b1 = rho1 * rho0, 2.0 * rho1 / half_width
    a2, b2 = rho2 * rho1, 2.0 * rho2 / half_width
    p, q = a1 * inverse + b1, -b1 * inverse
    k0 = inverse + p + a2 * p + b2
    k1 = q + a2 * q - b2 * (inverse + p)
    k2 = -b2 * q
    k0, k1, k2 = [jnp.broadcast_to(k, (8, 128)) for k in (k0, k1, k2)]
    for c in range(3):
        for z in range(BZ):
            def_o[c, z] = k0 * parts[0, c, z] + k1 * parts[1, c, z] + k2 * parts[2, c, z]
    for i in range(TILE_ROWS // 8):
        part = pl.ds(8 * i, 8)
        dem_o[part] = k0 * tiles[0, part] + k1 * tiles[1, part] + k2 * tiles[2, part]


def per_device(adjoint, linearized, stiffness, anchor, target_tile, target_row, target_col, offsets):
    vmem = lambda *shape, dtype=F32: pltpu.VMEM(shape, dtype)
    dma = pltpu.SemaphoreType.DMA
    ground = (BX, BY)
    operands = [
        pltpu.with_memory_space_constraint(x, pltpu.HBM)
        for x in (
            adjoint, linearized, stiffness, anchor,
            target_tile.reshape(ground), target_row.reshape(ground), target_col.reshape(ground),
            offsets.reshape((2,) + ground),
        )
    ]
    whole = pl.BlockSpec(memory_space=pltpu.VMEM)
    held = pl.pallas_call(
        kernel,
        out_shape=(
            pltpu.VMEM((3, 3, BZ, BX, BY), F32),
            pltpu.VMEM((3, TILE_ROWS, TILE_COLUMNS), F32),
            pltpu.VMEM((8, 128), F32),
        ),
        in_specs=[pl.BlockSpec(memory_space=pltpu.HBM)] * 8,
        out_specs=[whole] * 3,
        scratch_shapes=[
            vmem(6, BZ, BX, BY, dtype=BF16), vmem(18, BZ, BX, BY, dtype=BF16),
            vmem(BZ, BX, BY, dtype=BF16), vmem(BZ, BX, BY),
            vmem(*ground, dtype=jnp.int32), vmem(*ground, dtype=jnp.int32),
            vmem(*ground, dtype=jnp.int32), vmem(2, *ground),
            vmem(VARIABLES, AZ, 16, 256), vmem(8, 128), vmem(2, 16, 128),
            vmem(2, WZ, 16, 256), vmem(8, 128), vmem(2, 3, 16, 128),
            vmem(3, SZ, 16, 256), vmem(2, 8, 128), vmem(2, 4, 16, 128),
            vmem(4, 5, 8, 128),
            vmem(WZ, 16, 256), vmem(10, 16, 256),
            vmem(3, 12, 16, 256), vmem(3, 10, 16, 256),
            vmem(16, 3, 8, 128), vmem(32, 128), vmem(16, 128), vmem(1, 128),
            vmem(256, 4096, dtype=BF16), vmem(256, 4096, dtype=BF16), vmem(128, 4096),
            vmem(384, 4096, dtype=BF16), vmem(384, 4096, dtype=BF16),
            dma((8,)), dma((27,)), dma((27,)), dma((27,)), dma((27,)), dma((4,)), dma((4,)),
            dma((27,)), dma((27,)), dma((2,)), dma((2,)), dma, dma, dma, dma, dma, dma,
        ],
        compiler_params=pltpu.CompilerParams(
            collective_id=0, has_side_effects=True, vmem_limit_bytes=40 * 1024 * 1024
        ),
    )(*operands)
    return pl.pallas_call(
        combine,
        out_shape=(
            jax.ShapeDtypeStruct((3, BZ, BX, BY), F32),
            jax.ShapeDtypeStruct((TILE_ROWS, TILE_COLUMNS), F32),
        ),
        in_specs=[whole] * 3,
        out_specs=[whole] * 2,
    )(*[pltpu.with_memory_space_constraint(x, pltpu.VMEM) for x in held])


def solution(mesh):
    in_specs = (
        P(None, "gz", "gx", "gy"),
        P(None, "gz", "gx", "gy"),
        P("gz", "gx", "gy"),
        P("gz", "gx", "gy"),
        P("gx", "gy", None, None),
        P("gx", "gy", None),
        P("gx", "gy", None),
        P(None, "gx", "gy", None),
    )
    out_specs = (P(None, "gz", "gx", "gy"), P("gy", "gx"))
    return jax.shard_map(per_device, mesh=mesh, in_specs=in_specs, out_specs=out_specs, check_vma=False)
```

```python
import functools
import itertools

import jax
import jax.numpy as jnp
from jax import lax
from jax.experimental import pallas as pl
from jax.experimental.pallas import tpu as pltpu
from jax.sharding import PartitionSpec as P

MESH = pl.DeviceIdType.MESH
F32, BF16 = jnp.float32, jnp.bfloat16
NX, NY, NZ = 16, 8, 4
BZ, BX, BY = 8, 8, 128
TILE_ROWS, TILE_COLUMNS = 256, 128
VARIABLES = 6
SZ, WZ, AZ = 13, 11, 9
EDGE_Z, INNER_Z = (5, 6, 7, 0, 1), (2, 3, 4)

NEAR = [d for d in itertools.product((-1, 0, 1), repeat=3) if d != (0, 0, 0)]
PLANE = sorted(
    [(b, c) for b in range(NY) for c in range(NZ) if (b, c) != (0, 0)],
    key=lambda d: -(min(d[0], NY - d[0]) // 2 + min(d[1], NZ - d[1])),
)
DOWN = [d for d in NEAR if max(d) <= 0]
UP = [d for d in NEAR if min(d) >= 0]
SIDES = [d for d in NEAR if max(d) > 0]
COLLECTORS = [(b, c) for b in range(1, NY, 2) for c in range(0, NZ, 2)]
IMAGES_FIRST = 1
ROOTS = 4
SERVED = ((13, 14, 15), (), (9, 10, 11, 12), (4, 5, 6, 7, 8))
GROUND = [(a, b, c) for a in (0, 1) for b in (0, 1) for c in range(NZ)]


def near_index(d):
    return (d[0] + 1) * 9 + (d[1] + 1) * 3 + d[2] + 1


def guarded(condition, act):
    if condition is None:
        act()
    else:
        pl.when(condition)(act)


def rows_between(dx, below, above):
    if dx == 0:
        return pl.ds(0, 8), pl.ds(0, 8)
    if dx == 1:
        return pl.ds(8 - below, below), pl.ds(16 - below, below)
    return pl.ds(0, above), pl.ds(8, above)


def layers_between(dz, below, above):
    if dz == 0:
        return pl.ds(0, BZ), pl.ds(below, BZ)
    if dz == 1:
        return pl.ds(BZ - below, below), pl.ds(0, below)
    return pl.ds(0, above), pl.ds(below + BZ, above)


def sweep_factors(maxima):
    top = jnp.broadcast_to(jnp.max(maxima, axis=1, keepdims=True), (8, 128))
    low = top / 30.0
    center = 0.5 * (top + low)
    half_width = 0.5 * (top - low)
    ratio = center / half_width
    rho0 = 1.0 / ratio
    rho1 = 1.0 / (2.0 * ratio - rho0)
    rho2 = 1.0 / (2.0 * ratio - rho1)
    inverse = 1.0 / center
    a1, b1 = rho1 * rho0, 2.0 * rho1 / half_width
    a2, b2 = rho2 * rho1, 2.0 * rho2 / half_width
    p, q = a1 * inverse + b1, -b1 * inverse
    return inverse + p + a2 * p + b2, q + a2 * q - b2 * (inverse + p), -b2 * q


def kernel(
    adj_h, lin_h, stiff_h, anchor_h, tile_h, row_h, col_h, off_h,
    parts_o, tiles_o, factors_o,
    adj_v, lin_v, stiff_v, anchor_v, tile_v, row_v, col_v, off_v,
    AX, PA, PAE, WX, PW, PWE, EX, PS, PSE, TE, TG, W16, DG, G, K1, CE, CS, P1, P2, P3,
    RH, RL, CH, CL,
    load_sem, w_send, w_recv, a_send, a_recv, t_send, t_recv, s_send, s_recv,
    e_send, e_recv, p1_send, p1_recv, p2_send, p2_recv, p3_send, p3_recv,
):
    gx, gy, gz = lax.axis_index("gx"), lax.axis_index("gy"), lax.axis_index("gz")

    def at(dx, dy, dz):
        return (gx + dx, lax.rem(gy + dy + NY, NY), lax.rem(gz + dz + NZ, NZ))

    not_first, not_last, is_root = gx > 0, gx < NX - 1, gx < ROOTS
    is_collector = (lax.rem(gy, 2) == 1) & (lax.rem(gz, 2) == 0)
    can_send = {0: None, 1: not_last, -1: not_first}
    can_receive = {0: None, 1: not_first, -1: not_last}

    loads = [
        pltpu.make_async_copy(h, v, load_sem.at[i])
        for i, (h, v) in enumerate(
            ((stiff_h, stiff_v), (anchor_h, anchor_v), (adj_h, adj_v), (tile_h, tile_v),
             (row_h, row_v), (col_h, col_v), (off_h, off_v), (lin_h, lin_v))
        )
    ]
    for copy in loads[:2]:
        copy.start()

    barrier = pltpu.get_barrier_semaphore()

    def greet(device):
        pl.semaphore_signal(barrier, inc=1, device_id=device, device_id_type=MESH)

    def greet_near(steps):
        for dx in (0, 1, -1):
            these = [d for d in steps if d[0] == dx]

            def go(these=these):
                for d in these:
                    greet(at(*d))

            guarded(can_send[dx], go)

    greet_near(DOWN)
    greet_near(SIDES)

    @pl.when(is_collector)
    def _():
        for b, c in PLANE:
            if (0, (b + 1) % NY - 1, (c + 1) % NZ - 1) not in NEAR:
                greet(at(0, b, c))

    @pl.when(is_root)
    def _():
        for i in range(1, NX):
            greet((lax.rem(gx + i, NX), gy + 1 - lax.rem(gy, 2), gz - lax.rem(gz, 2)))

    for copy in loads[2:]:
        copy.start()

    lane = lax.broadcasted_iota(jnp.int32, (8, 128), 1)

    loads[0].wait()
    loads[1].wait()
    packed = jnp.zeros((8, 128), F32)
    for f, source in enumerate((stiff_v, anchor_v)):
        values = source[...].astype(F32)
        WX[f, 2:10, 0:8, 0:128] = values
        for z in range(BZ):
            w = f * BZ + z
            packed = jnp.where(lane // 8 == w, pltpu.roll(values[z], (8 * w + 4) % 128, 1), packed)
    PW[...] = packed

    pl.semaphore_wait(
        barrier,
        8 + jnp.where(not_first, 9, 0) + jnp.where(not_last, 9, 0)
        + len(COLLECTORS) - (2 - lax.rem(gy, 2)) * (1 + lax.rem(gz, 2))
        + jnp.where(is_collector, jnp.where(is_root, 4 * ROOTS - 4, 4 * ROOTS), 0),
    )

    def w_copy(d, fields=slice(0, 2), below=2):
        dx, dy, dz = d
        rs, rd = rows_between(dx, below, 1)
        if dy == 0:
            zs, zd = layers_between(dz, below, 1)
            zs, zd = pl.ds(2 + zs.start, zs.size), pl.ds(2 - below + zd.start, zd.size)
            src, dst = WX.at[fields, zs, rs, 0:128], WX.at[fields, zd, rd, 0:128]
        else:
            src, dst = PW.at[rs], PWE.at[0 if dy == 1 else 1, 1 - dz, rd]
        i = near_index(d) if fields != slice(1, 2) else 27 + near_index(d)
        return pltpu.make_async_remote_copy(
            src, dst, w_send.at[i], w_recv.at[i], device_id=at(*d), device_id_type=MESH
        )

    def a_copy(d):
        dx, dy, dz = d
        rs, rd = (pl.ds(0, 8), pl.ds(0, 8)) if dx == 0 else (pl.ds(0, 1), pl.ds(8, 1))
        if dy == 0:
            zs, zd = (pl.ds(0, 8), pl.ds(0, 8)) if dz == 0 else (pl.ds(0, 1), pl.ds(8, 1))
            src, dst = AX.at[:, zs, rs, 0:128], AX.at[:, zd, rd, 0:128]
        else:
            src, dst = PA.at[rs], PAE.at[-dz, rd]
        i = near_index(d)
        return pltpu.make_async_remote_copy(
            src, dst, a_send.at[i], a_recv.at[i], device_id=at(*d), device_id_type=MESH
        )

    def t_copy(a, b):
        i = 2 * a + b
        return pltpu.make_async_remote_copy(
            TE.at[0], TE.at[i], t_send.at[i], t_recv.at[i], device_id=at(a, b, 0), device_id_type=MESH
        )

    w_up = [(d[0], w_copy(d, slice(0, 1)) if d[1] == 0 else w_copy(d)) for d in UP]
    w_rest = [(d[0], w_copy(d)) for d in NEAR if d not in UP]
    w_rest += [(d[0], w_copy(d, slice(1, 2), 1)) for d in UP if d[1] == 0]
    a_copies = [(d[0], a_copy(d)) for d in DOWN]
    t_copies = [(a, t_copy(a, b)) for a, b in ((0, 1), (1, 0), (1, 1))]

    def start_all(copies):
        for step in (0, 1, -1):
            these = [c for dx, c in copies if dx == step]

            def go(these=these):
                for c in these:
                    c.start()

            guarded(can_send[step], go)

    def receive_all(copies):
        for step in (0, 1, -1):
            these = [c for dx, c in copies if dx == step]

            def go(these=these):
                for c in these:
                    c.wait_recv()

            guarded(can_receive[step], go)

    def sent_all(copies):
        for step in (0, 1, -1):
            these = [c for dx, c in copies if dx == step]

            def go(these=these):
                for c in these:
                    c.wait_send()

            guarded(can_send[step], go)

    start_all(w_up)

    loads[2].wait()
    packed = jnp.zeros((8, 128), F32)
    for v in range(VARIABLES):
        values = adj_v[v].astype(F32)
        AX[v, 0:8, 0:8, 0:128] = values
        for z in range(BZ):
            w = v * BZ + z
            packed = jnp.where(lane == w, pltpu.roll(values[z], w, 1), packed)
    PA[...] = packed

    for i in range(3, 7):
        loads[i].wait()
    TE[0, 0] = tile_v[...].astype(F32)
    TE[0, 1] = row_v[...].astype(F32)
    TE[0, 2] = col_v[...].astype(F32)
    TE[0, 3] = off_v[0]
    TE[0, 4] = off_v[1]

    start_all(a_copies)
    start_all(w_rest)
    start_all(t_copies)

    row16 = lax.broadcasted_iota(jnp.int32, (16, 256), 0)
    lane256 = lax.broadcasted_iota(jnp.int32, (16, 256), 1)
    ex = gx * BX + jnp.where(row16 < 12, row16, row16 - 16)
    ey = gy * BY + jnp.where(lane256 < 192, lane256, lane256 - 256)
    node_xy = (ex >= 0) & (ex <= NX * BX - 1) & (ey >= 0) & (ey <= NY * BY - 1)
    element_xy = (ex >= 0) & (ex <= NX * BX - 2) & (ey >= 0) & (ey <= NY * BY - 2)

    def node_mask(z):
        ez = gz * BZ + z
        return node_xy & (ez >= 0) & (ez <= NZ * BZ - 1)

    def element_mask(z):
        ez = gz * BZ + z
        return element_xy & (ez >= 0) & (ez <= NZ * BZ - 2)

    window16 = lax.broadcasted_iota(jnp.int32, (16, 128), 1)
    from_left = lax.rem(window16, 8) < 4

    receive_all(w_up)
    row8 = lax.broadcasted_iota(jnp.int32, (8, 128), 0)
    here_x, here_y = gx * BX + row8 <= NX * BX - 2, gy * BY + lane <= NY * BY - 2
    held, highest = None, jnp.zeros((8, 128), F32)
    for z in range(-1, BZ):
        slot, zz = (0, z + 8) if z < 0 else (1, z)
        shift = (124 - 8 * zz) % 128
        there = (gz * BZ + z >= 0) & (gz * BZ + z <= NZ * BZ - 2)
        main = jnp.where(here_x & here_y & there, WX[0, z + 2, 0:8, 0:128], 0.0)
        side = jnp.where(here_x & (gy > 0) & there, pltpu.roll(PWE[0, slot, 0:8], shift, 1), 0.0)
        under = jnp.where(here_y[0:1] & not_first & there, WX[0, z + 2, 12:16, 0:128][3:4], 0.0)
        corner = jnp.where(not_first & (gy > 0) & there, pltpu.roll(PWE[0, slot, 12:16], shift, 1)[3:4], 0.0)
        main = main + jnp.where(row8 == 0, under, pltpu.roll(main, 1, 0))
        side = side + jnp.where(row8 == 0, corner, pltpu.roll(side, 1, 0))
        layer = main + jnp.where(lane == 0, pltpu.roll(side, 1, 1), pltpu.roll(main, 1, 1))
        if held is not None:
            highest = jnp.maximum(highest, anchor_v[z] + 2.75 * (held + layer))
        held = layer

    mine_in_plane = pl.ds(gy * NZ + gz, 1)
    P1[mine_in_plane] = jnp.max(highest, axis=0, keepdims=True)
    for b, c in COLLECTORS:
        tell = pltpu.make_async_remote_copy(
            P1.at[mine_in_plane], P1.at[mine_in_plane], p1_send, p1_recv, device_id=(gx, b, c), device_id_type=MESH
        )
        pl.when((gy != b) | (gz != c))(tell.start)

    receive_all(a_copies)
    loads[7].wait()
    averages = []
    for v in range(VARIABLES):
        layers = []
        for z in range(BZ + 1):
            slot, zz = (0, z) if z < 8 else (1, 0)
            side = pltpu.roll(PAE[slot], (128 - (v * BZ + zz)) % 128, 1)
            layers.append(jnp.concatenate([AX[v, z, :, 0:128], side], axis=1))
        for z in range(BZ):
            total = layers[z] + layers[z + 1]
            total = total + pltpu.roll(total, 15, 0)
            total = total[0:8]
            total = total + pltpu.roll(total, 255, 1)
            AX[v, z, 0:8, 128:256] = total[:, 0:128] * (0.125 * 0.25)
    packs = [jnp.zeros((8, 128), F32), jnp.zeros((8, 128), F32)]
    for c in range(3):
        for z in range(BZ):
            total = lin_v[c, z].astype(F32) * AX[0, z, 0:8, 128:256]
            for v in range(1, VARIABLES):
                total = total + lin_v[3 * v + c, z].astype(F32) * AX[v, z, 0:8, 128:256]
            EX[c, z + 3, 0:8, 0:128] = total
            if z in EDGE_Z:
                t, w = 0, c * 5 + EDGE_Z.index(z)
            else:
                t, w = 1, c * 3 + INNER_Z.index(z)
            packs[t] = jnp.where(lane // 8 == w, pltpu.roll(total, (8 * w + 4) % 128, 1), packs[t])
    PS[0] = packs[0]
    PS[1] = packs[1]

    def s_copy(d):
        dx, dy, dz = d
        rs, rd = rows_between(dx, 3, 2)
        if dy == 0:
            zs, zd = layers_between(dz, 3, 2)
            src = EX.at[:, pl.ds(3 + zs.start, zs.size), rs, 0:128]
            dst = EX.at[:, zd, rd, 0:128]
        else:
            side = 0 if dy == 1 else 1
            if dz == 0:
                src, dst = PS.at[:, rs], PSE.at[side, pl.ds(1, 2), rd]
            else:
                src, dst = PS.at[0, rs], PSE.at[side, 0 if dz == 1 else 3, rd]
        i = near_index(d)
        return pltpu.make_async_remote_copy(
            src, dst, s_send.at[i], s_recv.at[i], device_id=at(*d), device_id_type=MESH
        )

    s_copies = [(d[0], s_copy(d)) for d in sorted(NEAR, key=lambda d: abs(d[1]))]
    start_all(s_copies)

    receive_all(w_rest)
    for f in range(2):
        for z in range(-2, 9):
            slot, zz = (0, z + 8) if z < 0 else (1, z) if z < 8 else (2, z - 8)
            mixed = jnp.where(from_left, PWE[0, slot], PWE[1, slot])
            w = f * BZ + zz
            WX[f, z + 2, :, 128:256] = pltpu.roll(mixed, (124 - 8 * w) % 128, 1)
    for z in range(-2, 9):
        W16[z + 2] = jnp.where(element_mask(z), WX[0, z + 2], 0.0) * (1.0 / 16.0)
    for z in range(-1, 9):
        total = W16[z + 1] + W16[z + 2]
        total = total + pltpu.roll(total, 1, 0)
        total = total + pltpu.roll(total, 1, 1)
        spring = jnp.where(node_mask(z), WX[1, z + 2], 0.0)
        DG[z + 1] = spring + 4.0 * total

    receive_all(t_copies)
    mine = (gx * NY + gy).astype(F32)
    rows = lax.broadcasted_iota(jnp.int32, (256, 128), 0).astype(F32).astype(BF16)
    nothing = jnp.zeros((256, 128), BF16)

    def halves(value):
        high = value.astype(BF16)
        return high, (value - high.astype(F32)).astype(BF16)

    for q in range(4):
        here = TE[q, 0] == mine
        if q >= 2:
            here = here & not_first
        row_at = jnp.where(here, TE[q, 1], -9.0)
        TG[q, 0] = jnp.where(here, TE[q, 2], -9.0)
        fr = jnp.where(here, TE[q, 3], 0.0)
        TG[q, 1] = jnp.where(here, TE[q, 4], 0.0)
        at0, at1 = row_at.astype(BF16), (row_at + 1.0).astype(BF16)
        (h0, l0), (h1, l1) = halves(1.0 - fr), halves(fr)
        for x in range(BX):
            part = pl.ds((q * BX + x) * 128, 128)
            one, two = rows == at0[x : x + 1], rows == at1[x : x + 1]
            RH[:, part] = jnp.where(one, h0[x : x + 1], jnp.where(two, h1[x : x + 1], nothing))
            RL[:, part] = jnp.where(one, l0[x : x + 1], jnp.where(two, l1[x : x + 1], nothing))

    own = pl.ds(gx, 1)
    ups = [
        pltpu.make_async_remote_copy(
            P2.at[own], P2.at[own], p2_send, p2_recv, device_id=(r, gy - b, gz + c), device_id_type=MESH
        )
        for b in (0, 1) for c in (0, 1) for r in range(ROOTS)
    ]

    @pl.when(is_collector)
    def _():
        pltpu.make_async_copy(P1.at[pl.ds(1, 31)], P1.at[pl.ds(1, 31)], p1_recv).wait()
        P2[own] = jnp.max(P1[...], axis=0, keepdims=True)
        for i in sorted(range(4 * ROOTS), key=lambda i: i % ROOTS):
            if i < ROOTS:
                pl.when(gx != i)(ups[i].start)
            else:
                ups[i].start()

    receive_all(s_copies)
    for side_slot in range(1):
        mixed = [jnp.where(from_left, PSE[0, s], PSE[1, s]) for s in range(4)]
        for c in range(3):
            for z in range(-3, 10):
                zz = z % 8
                if zz in EDGE_Z:
                    slot, w = (0 if z < 0 else 3 if z >= 8 else 1), c * 5 + EDGE_Z.index(zz)
                else:
                    slot, w = 2, c * 3 + INNER_Z.index(zz)
                EX[c, z + 3, :, 128:256] = pltpu.roll(mixed[slot], (124 - 8 * w) % 128, 1)

    def ahead_x(value):
        return pltpu.roll(value, 15, 0)

    def ahead_y(value):
        return pltpu.roll(value, 255, 1)

    def behind_x(value):
        return pltpu.roll(value, 1, 0)

    def behind_y(value):
        return pltpu.roll(value, 1, 1)

    held = None
    for z in range(-3, 10):
        mask = element_mask(z)
        sense = [jnp.where(mask, EX[c, z + 3], 0.0) for c in range(3)]
        if held is not None:
            qx, qy, qz = held[0] + sense[0], held[1] + sense[1], held[2] - sense[2]
            qx, qy, qz = behind_x(qx) - qx, behind_x(qy) + qy, behind_x(qz) + qz
            G[0, z + 2] = behind_y(qx) + qx
            G[1, z + 2] = behind_y(qy) - qy
            G[2, z + 2] = behind_y(qz) + qz
            if 0 <= z < BZ:
                for c in range(3):
                    parts_o[0, c, z] = G[c, z + 2, 0:8, 0:128]
        held = sense

    def element_forces(low, high, weight):
        gradient, middle = [], []
        for c in range(3):
            a, b = high[c] + low[c], high[c] - low[c]
            a1, b1 = ahead_y(a), ahead_y(b)
            sy, dy, sz = a1 + a, a1 - a, b1 + b
            sy1, dy1, sz1 = ahead_x(sy), ahead_x(dy), ahead_x(sz)
            middle.append(sy1 + sy)
            gradient.append((sy1 - sy, dy1 + dy, sz1 + sz))
        trace = gradient[0][0] + gradient[1][1] + gradient[2][2]
        half = 0.5 * weight
        plus, minus = [], []
        for c in range(3):
            s = [
                weight * (2.0 * gradient[c][c] + trace if c == d else gradient[c][d] + gradient[d][c])
                for d in range(3)
            ]
            m = half * middle[c]
            q = behind_x(s[0] - m) - (s[0] + m)
            q2 = behind_x(s[1]) + s[1]
            q3 = behind_x(s[2]) + s[2]
            r1 = behind_y(q + q2) + (q - q2)
            r2 = behind_y(q3) + q3
            plus.append(r1 + r2)
            minus.append(r1 - r2)
        return plus, minus

    held = None
    for j in range(11):
        plus, minus = element_forces([G[c, j] for c in range(3)], [G[c, j + 1] for c in range(3)], W16[j])
        if held is not None:
            for c in range(3):
                value = held[c] + minus[c] + DG[j - 1] * G[c, j]
                K1[c, j - 1] = value
                if 0 <= j - 2 < BZ:
                    parts_o[1, c, j - 2] = value[0:8, 0:128]
        held = plus

    sums = [jnp.zeros((8, 128), F32) for _ in range(3)]
    held = None
    for j in range(9):
        plus, minus = element_forces([K1[c, j] for c in range(3)], [K1[c, j + 1] for c in range(3)], W16[j + 1])
        if held is not None:
            z = j - 1
            for c in range(3):
                value = held[c] + minus[c] + DG[j] * K1[c, j]
                parts_o[2, c, z] = value[0:8, 0:128]
            share = ((NZ * BZ - 1 - z) - gz * BZ).astype(F32) * (1.0 / (NZ * BZ - 1))
            for k in range(3):
                sums[k] = sums[k] + share * parts_o[k, 2, z]
        held = plus
    for k in range(3):
        CE[0, k] = sums[k]

    def e_copy(a, b, c):
        i = a * 8 + b * 4 + c
        return pltpu.make_async_remote_copy(
            CE.at[0], CE.at[i], e_send.at[a], e_recv.at[a], device_id=at(a, b, c), device_id_type=MESH
        )

    for a in (0, 1):
        these = [e_copy(*d) for d in GROUND if d[0] == a and d != (0, 0, 0)]

        def go(these=these):
            for copy in these:
                copy.start()

        guarded(can_send[a], go)

    def wait_rows(count, semaphore):
        pltpu.make_async_copy(P1.at[pl.ds(0, count)], P1.at[pl.ds(0, count)], semaphore).wait()

    def root_step():
        pl.when(is_collector)(lambda: wait_rows(NX - 1, p2_recv))
        pl.when(jnp.logical_not(is_collector))(lambda: wait_rows(NX, p2_recv))
        P3[...] = jnp.max(P2[...], axis=0, keepdims=True)
        for r, served in enumerate(SERVED):

            @pl.when(gx == r)
            def _(served=served):
                for i in served:
                    pltpu.make_async_remote_copy(
                        P3, P3, p3_send, p3_recv, device_id=(i, gy, gz), device_id_type=MESH
                    ).start()

    images_first = gx < IMAGES_FIRST

    pl.when(is_root & jnp.logical_not(images_first))(root_step)

    pltpu.make_async_copy(CE.at[pl.ds(1, 7)], CE.at[pl.ds(1, 7)], e_recv.at[0]).wait()

    @pl.when(not_first)
    def _():
        pltpu.make_async_copy(CE.at[pl.ds(8, 8)], CE.at[pl.ds(8, 8)], e_recv.at[1]).wait()

    for q in range(4):
        for k in range(3):
            column = CE[4 * q, k] + CE[4 * q + 1, k] + CE[4 * q + 2, k] + CE[4 * q + 3, k]
            CS[q, k] = column if q < 2 else jnp.where(not_first, column, 0.0)

    def times(a, b):
        return lax.dot_general(a, b, (((1,), (1,)), ((), ())), preferred_element_type=F32)

    def image(count, column_of):
        for q in range(4):
            fc = TG[q, 1]
            at0, at1 = TG[q, 0].astype(BF16), (TG[q, 0] + 1.0).astype(BF16)
            values = []
            for k in range(count):
                column = column_of(q, k)
                values.append(halves(column * (1.0 - fc)) + halves(column * fc))
            for x in range(BX):
                part = pl.ds((q * BX + x) * 128, 128)
                one, two = rows[0:128] == at0[x : x + 1], rows[0:128] == at1[x : x + 1]
                for k in range(count):
                    h0, l0, h1, l1 = [value[x : x + 1] for value in values[k]]
                    own = pl.ds(k * 128, 128)
                    CH[own, part] = jnp.where(one, h0, jnp.where(two, h1, nothing[0:128]))
                    CL[own, part] = jnp.where(one, l0, jnp.where(two, l1, nothing[0:128]))
        span = pl.ds(0, count * 128)
        return times(RH[...], CH[span]) + times(RH[...], CL[span]) + times(RL[...], CH[span])

    @pl.when(images_first)
    def _():
        tiles = image(3, lambda q, k: CS[q, k])
        for k in range(3):
            tiles_o[k] = tiles[:, k * 128 : k * 128 + 128]

    sent_all(w_up)
    sent_all(w_rest)
    sent_all(a_copies)
    sent_all(t_copies)
    sent_all(s_copies)
    @pl.when(is_collector)
    def _():
        wait_rows(len(COLLECTORS) - 1, p1_send)
        pl.when(is_root)(lambda: wait_rows(4 * ROOTS - 1, p2_send))
        pl.when(jnp.logical_not(is_root))(lambda: wait_rows(4 * ROOTS, p2_send))

    @pl.when(jnp.logical_not(is_collector))
    def _():
        wait_rows(len(COLLECTORS), p1_send)

    pltpu.make_async_copy(CE.at[pl.ds(1, 7)], CE.at[pl.ds(1, 7)], e_send.at[0]).wait()

    @pl.when(not_last)
    def _():
        pltpu.make_async_copy(CE.at[pl.ds(8, 8)], CE.at[pl.ds(8, 8)], e_send.at[1]).wait()

    pl.when(images_first)(root_step)

    @pl.when(jnp.logical_not(is_root))
    def _():
        pltpu.make_async_copy(P3, P3, p3_recv).wait()

    k0, k1, k2 = sweep_factors(jnp.broadcast_to(P3[...], (8, 128)))
    for i, k in enumerate((k0, k1, k2)):
        factors_o[i] = k
        factors_o[3 + i] = jnp.where(images_first, k, 1.0 if i == 0 else 0.0)

    @pl.when(jnp.logical_not(images_first))
    def _():
        tiles_o[0] = image(1, lambda q, k: k0 * CS[q, 0] + k1 * CS[q, 1] + k2 * CS[q, 2])
        tiles_o[1:3] = jnp.zeros((2, TILE_ROWS, TILE_COLUMNS), F32)

    @pl.when(is_root)
    def _():
        for r, served in enumerate(SERVED):
            if served:
                pl.when(gx == r)(functools.partial(wait_rows, len(served), p3_send))


def combine(parts, tiles, factors, def_o, dem_o):
    k0, k1, k2 = factors[0], factors[1], factors[2]
    for c in range(3):
        for z in range(BZ):
            def_o[c, z] = k0 * parts[0, c, z] + k1 * parts[1, c, z] + k2 * parts[2, c, z]
    k0, k1, k2 = factors[3], factors[4], factors[5]
    for i in range(TILE_ROWS // 8):
        part = pl.ds(8 * i, 8)
        dem_o[part] = k0 * tiles[0, part] + k1 * tiles[1, part] + k2 * tiles[2, part]


def per_device(adjoint, linearized, stiffness, anchor, target_tile, target_row, target_col, offsets):
    vmem = lambda *shape, dtype=F32: pltpu.VMEM(shape, dtype)
    dma = pltpu.SemaphoreType.DMA
    ground = (BX, BY)
    operands = [
        pltpu.with_memory_space_constraint(x, pltpu.HBM)
        for x in (
            adjoint, linearized, stiffness, anchor,
            target_tile.reshape(ground), target_row.reshape(ground), target_col.reshape(ground),
            offsets.reshape((2,) + ground),
        )
    ]
    whole = pl.BlockSpec(memory_space=pltpu.VMEM)
    held = pl.pallas_call(
        kernel,
        out_shape=(
            pltpu.VMEM((3, 3, BZ, BX, BY), F32),
            pltpu.VMEM((3, TILE_ROWS, TILE_COLUMNS), F32),
            pltpu.VMEM((6, 8, 128), F32),
        ),
        in_specs=[pl.BlockSpec(memory_space=pltpu.HBM)] * 8,
        out_specs=[whole] * 3,
        scratch_shapes=[
            vmem(6, BZ, BX, BY, dtype=BF16), vmem(18, BZ, BX, BY, dtype=BF16),
            vmem(BZ, BX, BY, dtype=BF16), vmem(BZ, BX, BY),
            vmem(*ground, dtype=jnp.int32), vmem(*ground, dtype=jnp.int32),
            vmem(*ground, dtype=jnp.int32), vmem(2, *ground),
            vmem(VARIABLES, AZ, 16, 256), vmem(8, 128), vmem(2, 16, 128),
            vmem(2, WZ, 16, 256), vmem(8, 128), vmem(2, 3, 16, 128),
            vmem(3, SZ, 16, 256), vmem(2, 8, 128), vmem(2, 4, 16, 128),
            vmem(4, 5, 8, 128), vmem(4, 2, 8, 128),
            vmem(WZ, 16, 256), vmem(10, 16, 256),
            vmem(3, 12, 16, 256), vmem(3, 10, 16, 256),
            vmem(16, 3, 8, 128), vmem(4, 3, 8, 128), vmem(32, 128), vmem(16, 128), vmem(1, 128),
            vmem(256, 4096, dtype=BF16), vmem(256, 4096, dtype=BF16),
            vmem(384, 4096, dtype=BF16), vmem(384, 4096, dtype=BF16),
            dma((8,)), dma((54,)), dma((54,)), dma((27,)), dma((27,)), dma((4,)), dma((4,)),
            dma((27,)), dma((27,)), dma((2,)), dma((2,)), dma, dma, dma, dma, dma, dma,
        ],
        compiler_params=pltpu.CompilerParams(
            collective_id=0, has_side_effects=True, vmem_limit_bytes=40 * 1024 * 1024
        ),
    )(*operands)
    return pl.pallas_call(
        combine,
        out_shape=(
            jax.ShapeDtypeStruct((3, BZ, BX, BY), F32),
            jax.ShapeDtypeStruct((TILE_ROWS, TILE_COLUMNS), F32),
        ),
        in_specs=[whole] * 3,
        out_specs=[whole] * 2,
    )(*[pltpu.with_memory_space_constraint(x, pltpu.VMEM) for x in held])


def solution(mesh):
    in_specs = (
        P(None, "gz", "gx", "gy"),
        P(None, "gz", "gx", "gy"),
        P("gz", "gx", "gy"),
        P("gz", "gx", "gy"),
        P("gx", "gy", None, None),
        P("gx", "gy", None),
        P("gx", "gy", None),
        P(None, "gx", "gy", None),
    )
    out_specs = (P(None, "gz", "gx", "gy"), P("gy", "gx"))
    return jax.shard_map(per_device, mesh=mesh, in_specs=in_specs, out_specs=out_specs, check_vma=False)
```

```python
import functools
import itertools

import jax
import jax.numpy as jnp
from jax import lax
from jax.experimental import pallas as pl
from jax.experimental.pallas import tpu as pltpu
from jax.sharding import PartitionSpec as P

MESH = pl.DeviceIdType.MESH
F32, BF16 = jnp.float32, jnp.bfloat16
NX, NY, NZ = 16, 8, 4
BZ, BX, BY = 8, 8, 128
TILE_ROWS, TILE_COLUMNS = 256, 128
VARIABLES = 6
SZ, WZ, AZ = 13, 11, 9
EDGE_Z, INNER_Z = (5, 6, 7, 0, 1), (2, 3, 4)

NEAR = [d for d in itertools.product((-1, 0, 1), repeat=3) if d != (0, 0, 0)]
PLANE = sorted(
    [(b, c) for b in range(NY) for c in range(NZ) if (b, c) != (0, 0)],
    key=lambda d: -(min(d[0], NY - d[0]) // 2 + min(d[1], NZ - d[1])),
)
DOWN = [d for d in NEAR if max(d) <= 0]
UP = [d for d in NEAR if min(d) >= 0]
SIDES = [d for d in NEAR if max(d) > 0]
COLLECTORS = [(b, c) for b in range(1, NY, 2) for c in range(0, NZ, 2)]
IMAGES_FIRST = 1
ROOTS = 4
SERVED = ((13, 14, 15), (), (9, 10, 11, 12), (4, 5, 6, 7, 8))
GROUND = [(a, b, c) for a in (0, 1) for b in (0, 1) for c in range(NZ)]


def near_index(d):
    return (d[0] + 1) * 9 + (d[1] + 1) * 3 + d[2] + 1


def guarded(condition, act):
    if condition is None:
        act()
    else:
        pl.when(condition)(act)


def rows_between(dx, below, above):
    if dx == 0:
        return pl.ds(0, 8), pl.ds(0, 8)
    if dx == 1:
        return pl.ds(8 - below, below), pl.ds(16 - below, below)
    return pl.ds(0, above), pl.ds(8, above)


def layers_between(dz, below, above):
    if dz == 0:
        return pl.ds(0, BZ), pl.ds(below, BZ)
    if dz == 1:
        return pl.ds(BZ - below, below), pl.ds(0, below)
    return pl.ds(0, above), pl.ds(below + BZ, above)


def sweep_factors(maxima):
    top = jnp.broadcast_to(jnp.max(maxima, axis=1, keepdims=True), (8, 128))
    low = top / 30.0
    center = 0.5 * (top + low)
    half_width = 0.5 * (top - low)
    ratio = center / half_width
    rho0 = 1.0 / ratio
    rho1 = 1.0 / (2.0 * ratio - rho0)
    rho2 = 1.0 / (2.0 * ratio - rho1)
    inverse = 1.0 / center
    a1, b1 = rho1 * rho0, 2.0 * rho1 / half_width
    a2, b2 = rho2 * rho1, 2.0 * rho2 / half_width
    p, q = a1 * inverse + b1, -b1 * inverse
    return inverse + p + a2 * p + b2, q + a2 * q - b2 * (inverse + p), -b2 * q


def kernel(
    adj_h, lin_h, stiff_h, anchor_h, tile_h, row_h, col_h, off_h,
    parts_o, tiles_o, factors_o,
    adj_v, lin_v, stiff_v, anchor_v, tile_v, row_v, col_v, off_v,
    AX, PA, PAE, WX, PW, PWE, EX, PS, PSE, TE, TG, W16, DG, G, K1, CE, CS, P1, P2, P3,
    RH, RL, CH, CL,
    load_sem, w_send, w_recv, a_send, a_recv, t_send, t_recv, s_send, s_recv,
    e_send, e_recv, p1_send, p1_recv, p2_send, p2_recv, p3_send, p3_recv,
):
    gx, gy, gz = lax.axis_index("gx"), lax.axis_index("gy"), lax.axis_index("gz")

    def at(dx, dy, dz):
        return (gx + dx, lax.rem(gy + dy + NY, NY), lax.rem(gz + dz + NZ, NZ))

    not_first, not_last, is_root = gx > 0, gx < NX - 1, gx < ROOTS
    is_collector = (lax.rem(gy, 2) == 1) & (lax.rem(gz, 2) == 0)
    can_send = {0: None, 1: not_last, -1: not_first}
    can_receive = {0: None, 1: not_first, -1: not_last}

    loads = [
        pltpu.make_async_copy(h, v, load_sem.at[i])
        for i, (h, v) in enumerate(
            ((stiff_h, stiff_v), (anchor_h, anchor_v), (adj_h, adj_v), (tile_h, tile_v),
             (row_h, row_v), (col_h, col_v), (off_h, off_v), (lin_h, lin_v))
        )
    ]
    for copy in loads[:2]:
        copy.start()

    barrier = pltpu.get_barrier_semaphore()

    def greet(device):
        pl.semaphore_signal(barrier, inc=1, device_id=device, device_id_type=MESH)

    def greet_near(steps):
        for dx in (0, 1, -1):
            these = [d for d in steps if d[0] == dx]

            def go(these=these):
                for d in these:
                    greet(at(*d))

            guarded(can_send[dx], go)

    greet_near(DOWN)
    greet_near(SIDES)

    @pl.when(is_collector)
    def _():
        for b, c in PLANE:
            if (0, (b + 1) % NY - 1, (c + 1) % NZ - 1) not in NEAR:
                greet(at(0, b, c))

    @pl.when(is_root)
    def _():
        for i in range(1, NX):
            greet((lax.rem(gx + i, NX), gy + 1 - lax.rem(gy, 2), gz - lax.rem(gz, 2)))

    for copy in loads[2:]:
        copy.start()

    lane = lax.broadcasted_iota(jnp.int32, (8, 128), 1)

    loads[0].wait()
    loads[1].wait()
    packed = jnp.zeros((8, 128), F32)
    for f, source in enumerate((stiff_v, anchor_v)):
        values = source[...].astype(F32)
        WX[f, 2:10, 0:8, 0:128] = values
        for z in range(BZ):
            w = f * BZ + z
            packed = jnp.where(lane // 8 == w, pltpu.roll(values[z], (8 * w + 4) % 128, 1), packed)
    PW[...] = packed

    pl.semaphore_wait(
        barrier,
        8 + jnp.where(not_first, 9, 0) + jnp.where(not_last, 9, 0)
        + len(COLLECTORS) - (2 - lax.rem(gy, 2)) * (1 + lax.rem(gz, 2))
        + jnp.where(is_collector, jnp.where(is_root, 4 * ROOTS - 4, 4 * ROOTS), 0),
    )

    def w_copy(d, fields=slice(0, 2), below=2):
        dx, dy, dz = d
        rs, rd = rows_between(dx, below, 1)
        if dy == 0:
            zs, zd = layers_between(dz, below, 1)
            zs, zd = pl.ds(2 + zs.start, zs.size), pl.ds(2 - below + zd.start, zd.size)
            src, dst = WX.at[fields, zs, rs, 0:128], WX.at[fields, zd, rd, 0:128]
        else:
            src, dst = PW.at[rs], PWE.at[0 if dy == 1 else 1, 1 - dz, rd]
        i = near_index(d) if fields != slice(1, 2) else 27 + near_index(d)
        return pltpu.make_async_remote_copy(
            src, dst, w_send.at[i], w_recv.at[i], device_id=at(*d), device_id_type=MESH
        )

    def a_copy(d):
        dx, dy, dz = d
        rs, rd = (pl.ds(0, 8), pl.ds(0, 8)) if dx == 0 else (pl.ds(0, 1), pl.ds(8, 1))
        if dy == 0:
            zs, zd = (pl.ds(0, 8), pl.ds(0, 8)) if dz == 0 else (pl.ds(0, 1), pl.ds(8, 1))
            src, dst = AX.at[:, zs, rs, 0:128], AX.at[:, zd, rd, 0:128]
        else:
            src, dst = PA.at[rs], PAE.at[-dz, rd]
        i = near_index(d)
        return pltpu.make_async_remote_copy(
            src, dst, a_send.at[i], a_recv.at[i], device_id=at(*d), device_id_type=MESH
        )

    def t_copy(a, b):
        i = 2 * a + b
        return pltpu.make_async_remote_copy(
            TE.at[0], TE.at[i], t_send.at[i], t_recv.at[i], device_id=at(a, b, 0), device_id_type=MESH
        )

    w_up = [(d[0], w_copy(d, slice(0, 1)) if d[1] == 0 else w_copy(d)) for d in sorted(UP, key=lambda d: -sum(d))]
    w_rest = [(d[0], w_copy(d)) for d in NEAR if d not in UP]
    w_rest += [(d[0], w_copy(d, slice(1, 2), 1)) for d in UP if d[1] == 0]
    a_copies = [(d[0], a_copy(d)) for d in sorted(DOWN, key=sum)]
    t_copies = [(a, t_copy(a, b)) for a, b in ((0, 1), (1, 0), (1, 1))]

    def start_all(copies):
        for step in (1, -1, 0):
            these = [c for dx, c in copies if dx == step]

            def go(these=these):
                for c in these:
                    c.start()

            guarded(can_send[step], go)

    def receive_all(copies):
        for step in (0, 1, -1):
            these = [c for dx, c in copies if dx == step]

            def go(these=these):
                for c in these:
                    c.wait_recv()

            guarded(can_receive[step], go)

    def sent_all(copies):
        for step in (0, 1, -1):
            these = [c for dx, c in copies if dx == step]

            def go(these=these):
                for c in these:
                    c.wait_send()

            guarded(can_send[step], go)

    start_all(w_up)

    loads[2].wait()
    packed = jnp.zeros((8, 128), F32)
    for v in range(VARIABLES):
        values = adj_v[v].astype(F32)
        AX[v, 0:8, 0:8, 0:128] = values
        for z in range(BZ):
            w = v * BZ + z
            packed = jnp.where(lane == w, pltpu.roll(values[z], w, 1), packed)
    PA[...] = packed

    for i in range(3, 7):
        loads[i].wait()
    TE[0, 0] = tile_v[...].astype(F32)
    TE[0, 1] = row_v[...].astype(F32)
    TE[0, 2] = col_v[...].astype(F32)
    TE[0, 3] = off_v[0]
    TE[0, 4] = off_v[1]

    start_all(a_copies)
    start_all(w_rest)
    start_all(t_copies)

    row16 = lax.broadcasted_iota(jnp.int32, (16, 256), 0)
    lane256 = lax.broadcasted_iota(jnp.int32, (16, 256), 1)
    ex = gx * BX + jnp.where(row16 < 12, row16, row16 - 16)
    ey = gy * BY + jnp.where(lane256 < 192, lane256, lane256 - 256)
    node_xy = (ex >= 0) & (ex <= NX * BX - 1) & (ey >= 0) & (ey <= NY * BY - 1)
    element_xy = (ex >= 0) & (ex <= NX * BX - 2) & (ey >= 0) & (ey <= NY * BY - 2)

    def node_mask(z):
        ez = gz * BZ + z
        return node_xy & (ez >= 0) & (ez <= NZ * BZ - 1)

    def element_mask(z):
        ez = gz * BZ + z
        return element_xy & (ez >= 0) & (ez <= NZ * BZ - 2)

    window16 = lax.broadcasted_iota(jnp.int32, (16, 128), 1)
    from_left = lax.rem(window16, 8) < 4

    receive_all(w_up)
    row8 = lax.broadcasted_iota(jnp.int32, (8, 128), 0)
    here_x, here_y = gx * BX + row8 <= NX * BX - 2, gy * BY + lane <= NY * BY - 2
    held, highest = None, jnp.zeros((8, 128), F32)
    for z in range(-1, BZ):
        slot, zz = (0, z + 8) if z < 0 else (1, z)
        shift = (124 - 8 * zz) % 128
        there = (gz * BZ + z >= 0) & (gz * BZ + z <= NZ * BZ - 2)
        main = jnp.where(here_x & here_y & there, WX[0, z + 2, 0:8, 0:128], 0.0)
        side = jnp.where(here_x & (gy > 0) & there, pltpu.roll(PWE[0, slot, 0:8], shift, 1), 0.0)
        under = jnp.where(here_y[0:1] & not_first & there, WX[0, z + 2, 12:16, 0:128][3:4], 0.0)
        corner = jnp.where(not_first & (gy > 0) & there, pltpu.roll(PWE[0, slot, 12:16], shift, 1)[3:4], 0.0)
        main = main + jnp.where(row8 == 0, under, pltpu.roll(main, 1, 0))
        side = side + jnp.where(row8 == 0, corner, pltpu.roll(side, 1, 0))
        layer = main + jnp.where(lane == 0, pltpu.roll(side, 1, 1), pltpu.roll(main, 1, 1))
        if held is not None:
            highest = jnp.maximum(highest, anchor_v[z] + 2.75 * (held + layer))
        held = layer

    mine_in_plane = pl.ds(gy * NZ + gz, 1)
    P1[mine_in_plane] = jnp.max(highest, axis=0, keepdims=True)
    for b, c in COLLECTORS:
        tell = pltpu.make_async_remote_copy(
            P1.at[mine_in_plane], P1.at[mine_in_plane], p1_send, p1_recv, device_id=(gx, b, c), device_id_type=MESH
        )
        pl.when((gy != b) | (gz != c))(tell.start)

    receive_all(a_copies)
    loads[7].wait()
    averages = []
    for v in range(VARIABLES):
        layers = []
        for z in range(BZ + 1):
            slot, zz = (0, z) if z < 8 else (1, 0)
            side = pltpu.roll(PAE[slot], (128 - (v * BZ + zz)) % 128, 1)
            layers.append(jnp.concatenate([AX[v, z, :, 0:128], side], axis=1))
        for z in range(BZ):
            total = layers[z] + layers[z + 1]
            total = total + pltpu.roll(total, 15, 0)
            total = total[0:8]
            total = total + pltpu.roll(total, 255, 1)
            AX[v, z, 0:8, 128:256] = total[:, 0:128] * (0.125 * 0.25)
    packs = [jnp.zeros((8, 128), F32), jnp.zeros((8, 128), F32)]
    for c in range(3):
        for z in range(BZ):
            total = lin_v[c, z].astype(F32) * AX[0, z, 0:8, 128:256]
            for v in range(1, VARIABLES):
                total = total + lin_v[3 * v + c, z].astype(F32) * AX[v, z, 0:8, 128:256]
            EX[c, z + 3, 0:8, 0:128] = total
            if z in EDGE_Z:
                t, w = 0, c * 5 + EDGE_Z.index(z)
            else:
                t, w = 1, c * 3 + INNER_Z.index(z)
            packs[t] = jnp.where(lane // 8 == w, pltpu.roll(total, (8 * w + 4) % 128, 1), packs[t])
    PS[0] = packs[0]
    PS[1] = packs[1]

    def s_copy(d):
        dx, dy, dz = d
        rs, rd = rows_between(dx, 3, 2)
        if dy == 0:
            zs, zd = layers_between(dz, 3, 2)
            src = EX.at[:, pl.ds(3 + zs.start, zs.size), rs, 0:128]
            dst = EX.at[:, zd, rd, 0:128]
        else:
            side = 0 if dy == 1 else 1
            if dz == 0:
                src, dst = PS.at[:, rs], PSE.at[side, pl.ds(1, 2), rd]
            else:
                src, dst = PS.at[0, rs], PSE.at[side, 0 if dz == 1 else 3, rd]
        i = near_index(d)
        return pltpu.make_async_remote_copy(
            src, dst, s_send.at[i], s_recv.at[i], device_id=at(*d), device_id_type=MESH
        )

    s_copies = [(d[0], s_copy(d)) for d in sorted(NEAR, key=lambda d: -sum(abs(x) for x in d))]
    start_all(s_copies)

    receive_all(w_rest)
    for f in range(2):
        for z in range(-2, 9):
            slot, zz = (0, z + 8) if z < 0 else (1, z) if z < 8 else (2, z - 8)
            mixed = jnp.where(from_left, PWE[0, slot], PWE[1, slot])
            w = f * BZ + zz
            WX[f, z + 2, :, 128:256] = pltpu.roll(mixed, (124 - 8 * w) % 128, 1)
    for z in range(-2, 9):
        W16[z + 2] = jnp.where(element_mask(z), WX[0, z + 2], 0.0) * (1.0 / 16.0)
    for z in range(-1, 9):
        total = W16[z + 1] + W16[z + 2]
        total = total + pltpu.roll(total, 1, 0)
        total = total + pltpu.roll(total, 1, 1)
        spring = jnp.where(node_mask(z), WX[1, z + 2], 0.0)
        DG[z + 1] = spring + 4.0 * total

    own = pl.ds(gx, 1)
    ups = [
        pltpu.make_async_remote_copy(
            P2.at[own], P2.at[own], p2_send, p2_recv, device_id=(r, gy - b, gz + c), device_id_type=MESH
        )
        for b in (0, 1) for c in (0, 1) for r in range(ROOTS)
    ]

    @pl.when(is_collector)
    def _():
        pltpu.make_async_copy(P1.at[pl.ds(1, 31)], P1.at[pl.ds(1, 31)], p1_recv).wait()
        P2[own] = jnp.max(P1[...], axis=0, keepdims=True)
        for i in sorted(range(4 * ROOTS), key=lambda i: i % ROOTS):
            if i < ROOTS:
                pl.when(gx != i)(ups[i].start)
            else:
                ups[i].start()

    receive_all(t_copies)
    mine = (gx * NY + gy).astype(F32)
    rows = lax.broadcasted_iota(jnp.int32, (256, 128), 0).astype(F32).astype(BF16)
    nothing = jnp.zeros((256, 128), BF16)

    def halves(value):
        high = value.astype(BF16)
        return high, (value - high.astype(F32)).astype(BF16)

    for q in range(4):
        here = TE[q, 0] == mine
        if q >= 2:
            here = here & not_first
        row_at = jnp.where(here, TE[q, 1], -9.0)
        TG[q, 0] = jnp.where(here, TE[q, 2], -9.0)
        fr = jnp.where(here, TE[q, 3], 0.0)
        TG[q, 1] = jnp.where(here, TE[q, 4], 0.0)
        at0, at1 = row_at.astype(BF16), (row_at + 1.0).astype(BF16)
        (h0, l0), (h1, l1) = halves(1.0 - fr), halves(fr)
        for x in range(BX):
            part = pl.ds((q * BX + x) * 128, 128)
            one, two = rows == at0[x : x + 1], rows == at1[x : x + 1]
            RH[:, part] = jnp.where(one, h0[x : x + 1], jnp.where(two, h1[x : x + 1], nothing))
            RL[:, part] = jnp.where(one, l0[x : x + 1], jnp.where(two, l1[x : x + 1], nothing))

    receive_all(s_copies)
    for side_slot in range(1):
        mixed = [jnp.where(from_left, PSE[0, s], PSE[1, s]) for s in range(4)]
        for c in range(3):
            for z in range(-3, 10):
                zz = z % 8
                if zz in EDGE_Z:
                    slot, w = (0 if z < 0 else 3 if z >= 8 else 1), c * 5 + EDGE_Z.index(zz)
                else:
                    slot, w = 2, c * 3 + INNER_Z.index(zz)
                EX[c, z + 3, :, 128:256] = pltpu.roll(mixed[slot], (124 - 8 * w) % 128, 1)

    def ahead_x(value):
        return pltpu.roll(value, 15, 0)

    def ahead_y(value):
        return pltpu.roll(value, 255, 1)

    def behind_x(value):
        return pltpu.roll(value, 1, 0)

    def behind_y(value):
        return pltpu.roll(value, 1, 1)

    held = None
    for z in range(-3, 10):
        mask = element_mask(z)
        sense = [jnp.where(mask, EX[c, z + 3], 0.0) for c in range(3)]
        if held is not None:
            qx, qy, qz = held[0] + sense[0], held[1] + sense[1], held[2] - sense[2]
            qx, qy, qz = behind_x(qx) - qx, behind_x(qy) + qy, behind_x(qz) + qz
            G[0, z + 2] = behind_y(qx) + qx
            G[1, z + 2] = behind_y(qy) - qy
            G[2, z + 2] = behind_y(qz) + qz
            if 0 <= z < BZ:
                for c in range(3):
                    parts_o[0, c, z] = G[c, z + 2, 0:8, 0:128]
        held = sense

    def element_forces(low, high, weight):
        gradient, middle = [], []
        for c in range(3):
            a, b = high[c] + low[c], high[c] - low[c]
            a1, b1 = ahead_y(a), ahead_y(b)
            sy, dy, sz = a1 + a, a1 - a, b1 + b
            sy1, dy1, sz1 = ahead_x(sy), ahead_x(dy), ahead_x(sz)
            middle.append(sy1 + sy)
            gradient.append((sy1 - sy, dy1 + dy, sz1 + sz))
        trace = gradient[0][0] + gradient[1][1] + gradient[2][2]
        half = 0.5 * weight
        plus, minus = [], []
        for c in range(3):
            s = [
                weight * (2.0 * gradient[c][c] + trace if c == d else gradient[c][d] + gradient[d][c])
                for d in range(3)
            ]
            m = half * middle[c]
            q = behind_x(s[0] - m) - (s[0] + m)
            q2 = behind_x(s[1]) + s[1]
            q3 = behind_x(s[2]) + s[2]
            r1 = behind_y(q + q2) + (q - q2)
            r2 = behind_y(q3) + q3
            plus.append(r1 + r2)
            minus.append(r1 - r2)
        return plus, minus

    held = None
    for j in range(11):
        plus, minus = element_forces([G[c, j] for c in range(3)], [G[c, j + 1] for c in range(3)], W16[j])
        if held is not None:
            for c in range(3):
                value = held[c] + minus[c] + DG[j - 1] * G[c, j]
                K1[c, j - 1] = value
                if 0 <= j - 2 < BZ:
                    parts_o[1, c, j - 2] = value[0:8, 0:128]
        held = plus

    sums = [jnp.zeros((8, 128), F32) for _ in range(3)]
    held = None
    for j in range(9):
        plus, minus = element_forces([K1[c, j] for c in range(3)], [K1[c, j + 1] for c in range(3)], W16[j + 1])
        if held is not None:
            z = j - 1
            for c in range(3):
                value = held[c] + minus[c] + DG[j] * K1[c, j]
                parts_o[2, c, z] = value[0:8, 0:128]
            share = ((NZ * BZ - 1 - z) - gz * BZ).astype(F32) * (1.0 / (NZ * BZ - 1))
            for k in range(3):
                sums[k] = sums[k] + share * parts_o[k, 2, z]
        held = plus
    for k in range(3):
        CE[0, k] = sums[k]

    def e_copy(a, b, c):
        i = a * 8 + b * 4 + c
        return pltpu.make_async_remote_copy(
            CE.at[0], CE.at[i], e_send.at[a], e_recv.at[a], device_id=at(a, b, c), device_id_type=MESH
        )

    for a in (1, 0):
        far = sorted(GROUND, key=lambda d: -(d[1] + min(d[2], NZ - d[2])))
        these = [e_copy(*d) for d in far if d[0] == a and d != (0, 0, 0)]

        def go(these=these):
            for copy in these:
                copy.start()

        guarded(can_send[a], go)

    def wait_rows(count, semaphore):
        pltpu.make_async_copy(P1.at[pl.ds(0, count)], P1.at[pl.ds(0, count)], semaphore).wait()

    def root_step():
        pl.when(is_collector)(lambda: wait_rows(NX - 1, p2_recv))
        pl.when(jnp.logical_not(is_collector))(lambda: wait_rows(NX, p2_recv))
        P3[...] = jnp.max(P2[...], axis=0, keepdims=True)
        for r, served in enumerate(SERVED):

            @pl.when(gx == r)
            def _(served=served):
                for i in served:
                    pltpu.make_async_remote_copy(
                        P3, P3, p3_send, p3_recv, device_id=(i, gy, gz), device_id_type=MESH
                    ).start()

    images_first = gx < IMAGES_FIRST

    pl.when(is_root & jnp.logical_not(images_first))(root_step)

    pltpu.make_async_copy(CE.at[pl.ds(1, 7)], CE.at[pl.ds(1, 7)], e_recv.at[0]).wait()

    @pl.when(not_first)
    def _():
        pltpu.make_async_copy(CE.at[pl.ds(8, 8)], CE.at[pl.ds(8, 8)], e_recv.at[1]).wait()

    for q in range(4):
        for k in range(3):
            column = CE[4 * q, k] + CE[4 * q + 1, k] + CE[4 * q + 2, k] + CE[4 * q + 3, k]
            CS[q, k] = column if q < 2 else jnp.where(not_first, column, 0.0)

    def times(a, b):
        return lax.dot_general(a, b, (((1,), (1,)), ((), ())), preferred_element_type=F32)

    def image(count, column_of):
        for q in range(4):
            fc = TG[q, 1]
            at0, at1 = TG[q, 0].astype(BF16), (TG[q, 0] + 1.0).astype(BF16)
            values = []
            for k in range(count):
                column = column_of(q, k)
                values.append(halves(column * (1.0 - fc)) + halves(column * fc))
            for x in range(BX):
                part = pl.ds((q * BX + x) * 128, 128)
                one, two = rows[0:128] == at0[x : x + 1], rows[0:128] == at1[x : x + 1]
                for k in range(count):
                    h0, l0, h1, l1 = [value[x : x + 1] for value in values[k]]
                    own = pl.ds(k * 128, 128)
                    CH[own, part] = jnp.where(one, h0, jnp.where(two, h1, nothing[0:128]))
                    CL[own, part] = jnp.where(one, l0, jnp.where(two, l1, nothing[0:128]))
        span = pl.ds(0, count * 128)
        return times(RH[...], CH[span]) + times(RH[...], CL[span]) + times(RL[...], CH[span])

    @pl.when(images_first)
    def _():
        tiles = image(3, lambda q, k: CS[q, k])
        for k in range(3):
            tiles_o[k] = tiles[:, k * 128 : k * 128 + 128]

    sent_all(w_up)
    sent_all(w_rest)
    sent_all(a_copies)
    sent_all(t_copies)
    sent_all(s_copies)
    @pl.when(is_collector)
    def _():
        wait_rows(len(COLLECTORS) - 1, p1_send)
        pl.when(is_root)(lambda: wait_rows(4 * ROOTS - 1, p2_send))
        pl.when(jnp.logical_not(is_root))(lambda: wait_rows(4 * ROOTS, p2_send))

    @pl.when(jnp.logical_not(is_collector))
    def _():
        wait_rows(len(COLLECTORS), p1_send)

    pltpu.make_async_copy(CE.at[pl.ds(1, 7)], CE.at[pl.ds(1, 7)], e_send.at[0]).wait()

    @pl.when(not_last)
    def _():
        pltpu.make_async_copy(CE.at[pl.ds(8, 8)], CE.at[pl.ds(8, 8)], e_send.at[1]).wait()

    pl.when(images_first)(root_step)

    @pl.when(jnp.logical_not(is_root))
    def _():
        pltpu.make_async_copy(P3, P3, p3_recv).wait()

    k0, k1, k2 = sweep_factors(jnp.broadcast_to(P3[...], (8, 128)))
    for i, k in enumerate((k0, k1, k2)):
        factors_o[i] = k
        factors_o[3 + i] = jnp.where(images_first, k, 1.0 if i == 0 else 0.0)

    @pl.when(jnp.logical_not(images_first))
    def _():
        tiles_o[0] = image(1, lambda q, k: k0 * CS[q, 0] + k1 * CS[q, 1] + k2 * CS[q, 2])
        tiles_o[1:3] = jnp.zeros((2, TILE_ROWS, TILE_COLUMNS), F32)

    @pl.when(is_root)
    def _():
        for r, served in enumerate(SERVED):
            if served:
                pl.when(gx == r)(functools.partial(wait_rows, len(served), p3_send))


def combine(parts, tiles, factors, def_o, dem_o):
    k0, k1, k2 = factors[0], factors[1], factors[2]
    for c in range(3):
        for z in range(BZ):
            def_o[c, z] = k0 * parts[0, c, z] + k1 * parts[1, c, z] + k2 * parts[2, c, z]
    k0, k1, k2 = factors[3], factors[4], factors[5]
    for i in range(TILE_ROWS // 8):
        part = pl.ds(8 * i, 8)
        dem_o[part] = k0 * tiles[0, part] + k1 * tiles[1, part] + k2 * tiles[2, part]


def per_device(adjoint, linearized, stiffness, anchor, target_tile, target_row, target_col, offsets):
    vmem = lambda *shape, dtype=F32: pltpu.VMEM(shape, dtype)
    dma = pltpu.SemaphoreType.DMA
    ground = (BX, BY)
    operands = [
        pltpu.with_memory_space_constraint(x, pltpu.HBM)
        for x in (
            adjoint, linearized, stiffness, anchor,
            target_tile.reshape(ground), target_row.reshape(ground), target_col.reshape(ground),
            offsets.reshape((2,) + ground),
        )
    ]
    whole = pl.BlockSpec(memory_space=pltpu.VMEM)
    held = pl.pallas_call(
        kernel,
        out_shape=(
            pltpu.VMEM((3, 3, BZ, BX, BY), F32),
            pltpu.VMEM((3, TILE_ROWS, TILE_COLUMNS), F32),
            pltpu.VMEM((6, 8, 128), F32),
        ),
        in_specs=[pl.BlockSpec(memory_space=pltpu.HBM)] * 8,
        out_specs=[whole] * 3,
        scratch_shapes=[
            vmem(6, BZ, BX, BY, dtype=BF16), vmem(18, BZ, BX, BY, dtype=BF16),
            vmem(BZ, BX, BY, dtype=BF16), vmem(BZ, BX, BY),
            vmem(*ground, dtype=jnp.int32), vmem(*ground, dtype=jnp.int32),
            vmem(*ground, dtype=jnp.int32), vmem(2, *ground),
            vmem(VARIABLES, AZ, 16, 256), vmem(8, 128), vmem(2, 16, 128),
            vmem(2, WZ, 16, 256), vmem(8, 128), vmem(2, 3, 16, 128),
            vmem(3, SZ, 16, 256), vmem(2, 8, 128), vmem(2, 4, 16, 128),
            vmem(4, 5, 8, 128), vmem(4, 2, 8, 128),
            vmem(WZ, 16, 256), vmem(10, 16, 256),
            vmem(3, 12, 16, 256), vmem(3, 10, 16, 256),
            vmem(16, 3, 8, 128), vmem(4, 3, 8, 128), vmem(32, 128), vmem(16, 128), vmem(1, 128),
            vmem(256, 4096, dtype=BF16), vmem(256, 4096, dtype=BF16),
            vmem(384, 4096, dtype=BF16), vmem(384, 4096, dtype=BF16),
            dma((8,)), dma((54,)), dma((54,)), dma((27,)), dma((27,)), dma((4,)), dma((4,)),
            dma((27,)), dma((27,)), dma((2,)), dma((2,)), dma, dma, dma, dma, dma, dma,
        ],
        compiler_params=pltpu.CompilerParams(
            collective_id=0, has_side_effects=True, vmem_limit_bytes=40 * 1024 * 1024
        ),
    )(*operands)
    return pl.pallas_call(
        combine,
        out_shape=(
            jax.ShapeDtypeStruct((3, BZ, BX, BY), F32),
            jax.ShapeDtypeStruct((TILE_ROWS, TILE_COLUMNS), F32),
        ),
        in_specs=[whole] * 3,
        out_specs=[whole] * 2,
    )(*[pltpu.with_memory_space_constraint(x, pltpu.VMEM) for x in held])


def solution(mesh):
    in_specs = (
        P(None, "gz", "gx", "gy"),
        P(None, "gz", "gx", "gy"),
        P("gz", "gx", "gy"),
        P("gz", "gx", "gy"),
        P("gx", "gy", None, None),
        P("gx", "gy", None),
        P("gx", "gy", None),
        P(None, "gx", "gy", None),
    )
    out_specs = (P(None, "gz", "gx", "gy"), P("gy", "gx"))
    return jax.shard_map(per_device, mesh=mesh, in_specs=in_specs, out_specs=out_specs, check_vma=False)
```
